32 devices in a mesh: groups: 2 (over x), dp: 16 (over z, y, core).
Axes of the slice: x: 2, y: 2, z: 4, core: 2. Of those that a mesh axis runs over, the one named last changes fastest.
Arguments:
- tokens: bfloat16 [4096, 8192], P(('groups', 'dp')), parts along dimension 0, may hold values from -6 to 6
- value_weight_matrix: bfloat16 [8192, 1024], P('dp'), may hold values from -0.0625 to 0.0625
- adapter_down_weight: bfloat16 [64, 64, 8192], P(None, None, 'dp'), may hold values from -0.0625 to 0.0625
- adapter_up_weight: bfloat16 [64, 64, 1024], P(None, None, 'dp'), may hold values from -0.75 to 0.75
- adapter_of_block: int32 [32], P('groups'), parts along dimension 0, may hold values from 0 to 63
- block_live_length: int32 [32], P(('groups', 'dp')), parts along dimension 0, may hold values from 1 to 128
Outputs:
- values: bfloat16 [4096, 1024], P(('groups', 'dp')), parts along dimension 0
The draws below stay inside these ranges and needn't reach their ends.
There are 2 independent parts, one for each index of `groups`. The reference program is written for one: setup_inputs(seed, part) draws one part's arguments, and reference() takes and returns one part's arrays. A program takes and returns all parts, laid end to end along the dimension named above; an argument that names none is the same for every part. Nothing has to cross between parts.
All inputs are finite; a program needn't handle non-finite values.
Results may differ from the reference program's by a relative error of at most 0.0034.
Values may be sent and summed in bfloat16 or wider, within the bound.
No kernel may reach another device: no remote copies, remote signals or barrier semaphores. Data moves between devices by JAX's collectives and lax.ppermute only.
A program may use at most 128 MiB of HBM per device.

```python
import math
import jax
import jax.numpy as jnp
import numpy as np
from jax import lax

MODEL_FEATURES = 8192
ADAPTER_RANK = 64
BLOCK = 128
VALUE_FEATURES = 1024
ADAPTER_COUNT = 64
BLOCKS = 16
ROWS = 2048


def place_ends(drawn, rng, least, largest):
    place = [jax.random.randint(jax.random.fold_in(rng, axis), (), 0, length) for axis, length in enumerate(drawn.shape)]
    main_axis = drawn.shape.index(max(drawn.shape))
    beside = place[:main_axis] + [(place[main_axis] + 1) % drawn.shape[main_axis]] + place[main_axis + 1:]
    return drawn.at[tuple(place)].set(least).at[tuple(beside)].set(largest)


def block_levels(key, extent, shards, smallest, largest):
    loudness, own = 1.0, jax.random.fold_in(key, 6)
    for dim, shards_of in shards:
        draws = jnp.exp(jax.random.uniform(jax.random.fold_in(own, dim), (shards_of,), jnp.float32, smallest / len(shards), largest / len(shards)))
        loudness = loudness * jnp.repeat(draws, extent[dim] // shards_of).reshape([-1 if axis == dim else 1 for axis in range(len(extent))])
    return loudness


def cumulative_ranks(amount, skew):
    weights = [(1 << 20) // math.isqrt(standing ** skew) + 1 for standing in range(1, amount + 1)]
    spread = 1 + sum(weights) // (1 << 30)
    return np.cumsum(np.array([max(1, weight // spread) for weight in weights]))


def skewed_ids(rng, extent, count, slope):
    listing = cumulative_ranks(count, slope)
    lot = jax.random.randint(jax.random.fold_in(rng, 1), extent, 0, int(listing[count - 1]))
    grade = jnp.searchsorted(jnp.asarray(listing, jnp.int32), lot, side="right")
    return jax.random.permutation(jax.random.fold_in(rng, 2), count)[grade].astype(jnp.int32)


def gaussian(rng, extent, deviation, reach, shards=(), kind=jnp.bfloat16):
    level = block_levels(rng, extent, shards, -0.22, 0.18) if shards else 1.0
    values = jax.random.normal(rng, extent, jnp.float32) * deviation * level
    return jnp.minimum(jnp.maximum(values, -reach), reach).astype(kind)


def setup_inputs(seed: int = 0, part: int = 0) -> dict:
    seeds = jax.random.split(jax.random.key(seed), 7)
    part_keys = jax.random.split(jax.random.fold_in(seeds[6], part), 7)
    tokens = gaussian(part_keys[0], (ROWS, MODEL_FEATURES), 1.0, 6.0, ((0, 16),))
    value_weight_matrix = gaussian(seeds[1], (MODEL_FEATURES, VALUE_FEATURES), MODEL_FEATURES ** -0.5, 0.0625, ((0, 16),))
    adapter_down_weight = gaussian(seeds[2], (ADAPTER_COUNT, ADAPTER_RANK, MODEL_FEATURES), MODEL_FEATURES ** -0.5, 0.0625, ((2, 16),))
    adapter_up_weight = gaussian(seeds[3], (ADAPTER_COUNT, ADAPTER_RANK, VALUE_FEATURES), ADAPTER_RANK ** -0.5, 0.75, ((2, 16),))
    adapter_of_block = place_ends(skewed_ids(part_keys[4], (BLOCKS,), ADAPTER_COUNT, 2), jax.random.fold_in(part_keys[4], 3), 0, ADAPTER_COUNT - 1).astype(jnp.int32)
    block_live_length = place_ends(jax.random.randint(part_keys[5], (BLOCKS,), 1, BLOCK + 1), jax.random.fold_in(part_keys[5], 1), 1, BLOCK).astype(jnp.int32)
    return dict(tokens=tokens, value_weight_matrix=value_weight_matrix, adapter_down_weight=adapter_down_weight, adapter_up_weight=adapter_up_weight, adapter_of_block=adapter_of_block, block_live_length=block_live_length)


ADAPTER_SCALE = 0.5


def reference(tokens, value_weight_matrix, adapter_down_weight, adapter_up_weight, adapter_of_block, block_live_length):
    base_out = jnp.dot(tokens, value_weight_matrix, preferred_element_type=jnp.float32)
    row_blocks = tokens.reshape(BLOCKS, BLOCK, MODEL_FEATURES)

    def one_block(inputs):
        block_rows, chosen_adapter = inputs
        down_lookup = jnp.take(adapter_down_weight, chosen_adapter, axis=0)
        up_lookup = jnp.take(adapter_up_weight, chosen_adapter, axis=0)
        narrowed_rows = jnp.dot(block_rows, down_lookup.T, preferred_element_type=jnp.float32)
        reduced_rank_output = (narrowed_rows * ADAPTER_SCALE).astype(jnp.bfloat16)
        return jnp.dot(reduced_rank_output, up_lookup, preferred_element_type=jnp.float32)

    change_rows = lax.map(one_block, (row_blocks, adapter_of_block.astype(jnp.int32)))
    change_rows = change_rows.reshape(ROWS, VALUE_FEATURES)
    live_rows = jnp.arange(BLOCK, dtype=jnp.int32)[None, :] < block_live_length[:, None]
    return jnp.where(live_rows.reshape(ROWS, 1), base_out + change_rows, 0.0).astype(jnp.bfloat16)
```

```python
import jax
import jax.numpy as jnp
from jax import lax
from jax.sharding import PartitionSpec as P

BLOCK = 128
SQUARE = 4
ADAPTER_SCALE = 0.5


def per_device(
    tokens,
    value_weight_matrix,
    adapter_down_weight,
    adapter_up_weight,
    adapter_of_block,
    block_live_length,
):
    group_count = lax.axis_size("groups")
    peer_count = lax.axis_size("dp")
    ring = peer_count // SQUARE
    depth, columns = value_weight_matrix.shape
    half = depth // 2
    rank = adapter_down_weight.shape[1]
    rows = tokens.shape[0]
    group, peer = lax.axis_index("groups"), lax.axis_index("dp")
    side = lax.rem(group, 2)
    place, member = peer // SQUARE, lax.rem(peer, SQUARE)

    across = [(g, g ^ 1) for g in range(group_count)]
    onward = [
        (p, (p // SQUARE + 1) % ring * SQUARE + p % SQUARE) for p in range(peer_count)
    ]

    def within(step):
        return [(p, p ^ step) for p in range(peer_count)]

    held = lax.dynamic_slice_in_dim(value_weight_matrix, side * half, half, 0)
    other = lax.dynamic_slice_in_dim(value_weight_matrix, (1 - side) * half, half, 0)
    weights = [(held, other)]
    for _ in range(ring - 1):
        held = lax.ppermute(held, "dp", onward)
        weights.append((held, lax.ppermute(held, "groups", across)))

    pieces = tokens.reshape(rows, ring, SQUARE, 2, half)
    order = lax.rem(place - jnp.arange(ring) + ring, ring)
    shares = []
    for step in range(SQUARE):
        share = lax.dynamic_index_in_dim(pieces, member ^ step, 2, keepdims=False)
        share = jnp.take(share, order, axis=1)
        share = jnp.take(share, jnp.stack([side, 1 - side]), axis=2)
        share = share.reshape(rows, ring, 2 * half)
        shares.append(share if step == 0 else lax.ppermute(share, "dp", within(step)))
    features = jnp.stack(shares)

    chosen = jnp.concatenate(
        [
            jnp.take(adapter_down_weight, adapter_of_block, axis=0),
            jnp.take(adapter_up_weight, adapter_of_block, axis=0),
        ],
        axis=2,
    )
    chosen = lax.all_to_all(chosen, "dp", 0, 0, tiled=True)
    shrunk = jnp.einsum(
        "nif,irf->nr",
        tokens.reshape(rows, peer_count, depth),
        chosen[:, :, :depth],
        preferred_element_type=jnp.float32,
    )
    low_rank = (shrunk * ADAPTER_SCALE).astype(jnp.bfloat16)
    up = jnp.swapaxes(chosen[:, :, depth:], 0, 1).reshape(rank, columns)
    change = jnp.dot(low_rank, up, preferred_element_type=jnp.float32)

    partial = jnp.zeros((SQUARE, rows, columns), jnp.float32)
    for step, pair in enumerate(weights):
        partial = partial + jnp.einsum(
            "bnf,fv->bnv",
            features[:, :, step],
            jnp.concatenate(pair),
            preferred_element_type=jnp.float32,
        )
    outgoing = jnp.stack([partial[1], partial[3]])
    incoming = lax.ppermute(outgoing, "dp", within(1))
    there = partial[2] + incoming[1]
    here = partial[0] + incoming[0]
    base = here + lax.ppermute(there, "dp", within(2))

    live_rows = jnp.arange(BLOCK, dtype=jnp.int32)[None, :] < block_live_length[:, None]
    return jnp.where(live_rows.reshape(-1, 1), base + change, 0.0).astype(jnp.bfloat16)


def solution(mesh):
    in_specs = (
        P(("groups", "dp"), None),
        P("dp", None),
        P(None, None, "dp"),
        P(None, None, "dp"),
        P("groups"),
        P(("groups", "dp")),
    )
    out_specs = P(("groups", "dp"), None)
    return jax.shard_map(
        per_device, mesh=mesh, in_specs=in_specs, out_specs=out_specs, check_vma=False
    )
```

```python
import functools

import jax
import jax.numpy as jnp
from jax import lax
from jax.experimental import pallas as pl
from jax.experimental.pallas import tpu as pltpu
from jax.sharding import PartitionSpec as P

BLOCK = 128
SQUARE = 4
CHUNKS = 2
LANES = 128
ADAPTER_SCALE = 0.5
VMEM_BYTES = 40 * 2**20

VMEM = pl.BlockSpec(memory_space=pltpu.VMEM)
SMEM = pl.BlockSpec(memory_space=pltpu.SMEM)
ANY = pl.BlockSpec(memory_space=pl.ANY)


def params():
    return pltpu.CompilerParams(vmem_limit_bytes=VMEM_BYTES)


def cost(flops, touched):
    return pl.CostEstimate(flops=flops, bytes_accessed=touched, transcendentals=0)


def share_kernel(ring, depth, where_ref, tokens_ref, *share_refs):
    place, member, side = where_ref[0], where_ref[1], where_ref[2]
    step = 2 * side - 1
    order = [0]
    for hop in range(1, ring // 2):
        order += [step * hop, -step * hop]
    order.append(ring // 2)
    for turn, ahead in enumerate(order):
        source = lax.rem(place + ahead + ring, ring)
        for mate, share_ref in enumerate(share_refs):
            start = pl.multiple_of((source * SQUARE + (member ^ mate)) * depth, depth)
            share_ref[:, turn * depth : (turn + 1) * depth] = tokens_ref[:, pl.ds(start, depth)]


def shares_of(where, tokens, ring, depth):
    rows, features = tokens.shape
    step = 32
    width = ring * depth
    return pl.pallas_call(
        functools.partial(share_kernel, ring, depth),
        grid=(rows // step,),
        in_specs=[SMEM, pl.BlockSpec((step, features), lambda i: (i, 0))],
        out_specs=[pl.BlockSpec((step, width), lambda i: (i, 0))] * SQUARE,
        out_shape=[jax.ShapeDtypeStruct((rows, width), tokens.dtype)] * SQUARE,
        compiler_params=params(),
        cost_estimate=cost(0, 4 * rows * features),
    )(where, tokens)


def packet_sizes(depth, rank, width):
    folds = min(LANES // width, rank // 16)
    return depth // LANES, folds, rank // folds


def packet_kernel(chosen_ref, down_ref, up_ref, packet_ref, down_held, up_held, sems):
    blocks, rank, depth = down_held.shape
    width = up_held.shape[2]
    groups, folds, high = packet_sizes(depth, rank, width)

    def copies(k):
        a = chosen_ref[k]
        return (
            pltpu.make_async_copy(down_ref.at[a], down_held.at[k], sems.at[0, k]),
            pltpu.make_async_copy(up_ref.at[a], up_held.at[k], sems.at[1, k]),
        )

    for k in range(blocks):
        for copy in copies(k):
            copy.start()
    for k in range(blocks):
        for copy in copies(k):
            copy.wait()
        for g in range(groups):
            packet_ref[k, g * rank : (g + 1) * rank, :] = down_held[
                k, :, g * LANES : (g + 1) * LANES
            ]
        parts = [up_held[k, f * high : (f + 1) * high, :] for f in range(folds)]
        if folds * width < LANES:
            parts.append(jnp.zeros((high, LANES - folds * width), packet_ref.dtype))
        packet_ref[k, groups * rank :, :] = jnp.concatenate(parts, axis=1)


def packets_of(adapter_of_block, down, up):
    blocks = adapter_of_block.shape[0]
    rank, depth, width = down.shape[1], down.shape[2], up.shape[2]
    groups, _, high = packet_sizes(depth, rank, width)
    tall = groups * rank + high
    return pl.pallas_call(
        packet_kernel,
        in_specs=[SMEM, ANY, ANY],
        out_specs=VMEM,
        out_shape=jax.ShapeDtypeStruct((blocks, tall, LANES), down.dtype),
        scratch_shapes=[
            pltpu.VMEM((blocks, rank, depth), down.dtype),
            pltpu.VMEM((blocks, rank, width), up.dtype),
            pltpu.SemaphoreType.DMA((2, blocks)),
        ],
        compiler_params=params(),
        cost_estimate=cost(0, 4 * blocks * tall * LANES),
    )(adapter_of_block, down, up)


def change_kernel(rank, depth, width, tokens_ref, packet_ref, change_ref, down_held, up_held):
    peers = packet_ref.shape[0]
    groups, folds, high = packet_sizes(depth, rank, width)
    for p in range(peers):
        for g in range(groups):
            start = p * depth + g * LANES
            down_held[:, start : start + LANES] = packet_ref[p, g * rank : (g + 1) * rank, :]
        for f in range(folds):
            up_held[f * high : (f + 1) * high, p * width : (p + 1) * width] = packet_ref[
                p, groups * rank :, f * width : (f + 1) * width
            ]
    shrunk = lax.dot_general(
        tokens_ref[...],
        down_held[...],
        (((1,), (1,)), ((), ())),
        preferred_element_type=jnp.float32,
    )
    low_rank = (shrunk * ADAPTER_SCALE).astype(jnp.bfloat16)
    change_ref[...] = jnp.dot(low_rank, up_held[...], preferred_element_type=jnp.float32)


def change_of(tokens, packets, rank, depth, width):
    rows, features = tokens.shape
    columns = packets.shape[0] * width
    return pl.pallas_call(
        functools.partial(change_kernel, rank, depth, width),
        in_specs=[VMEM, VMEM],
        out_specs=VMEM,
        out_shape=jax.ShapeDtypeStruct((rows, columns), jnp.float32),
        scratch_shapes=[
            pltpu.VMEM((rank, features), tokens.dtype),
            pltpu.VMEM((rank, columns), tokens.dtype),
        ],
        compiler_params=params(),
        cost_estimate=cost(2 * rows * rank * (features + columns), 2 * rows * features),
    )(tokens, packets)


def stacked(share_refs, turn, depth):
    return jnp.concatenate(
        [share[:, turn * depth : (turn + 1) * depth] for share in share_refs], axis=0
    )


def near_kernel(depth, *refs):
    shares, weights, total_ref = refs[:SQUARE], refs[SQUARE:-1], refs[-1]
    total = None
    for turn, weight in enumerate(weights):
        term = jnp.dot(
            stacked(shares, turn, depth), weight[...], preferred_element_type=jnp.float32
        )
        total = term if total is None else total + term
    total_ref[...] = total


def near_of(shares, own, chunk, pieces):
    depth = own.shape[0]
    rows = shares[0].shape[0] * SQUARE
    columns = own.shape[1] // CHUNKS
    return pl.pallas_call(
        functools.partial(near_kernel, depth),
        grid=(1,),
        in_specs=[pl.BlockSpec(shares[0].shape, lambda i: (0, 0))] * SQUARE
        + [pl.BlockSpec((depth, columns), lambda i: (0, chunk))]
        + [pl.BlockSpec((depth, columns), lambda i: (0, 0))] * len(pieces),
        out_specs=pl.BlockSpec((rows, columns), lambda i: (0, 0)),
        out_shape=jax.ShapeDtypeStruct((rows, columns), jnp.float32),
        compiler_params=params(),
        cost_estimate=cost(2 * rows * depth * columns * (1 + len(pieces)), 2**22),
    )(*shares, own, *pieces)


def far_kernel(
    depth, where_ref, s0, s1, s2, s3, total_ref, held_ref, other_ref, out_ref, keep_ref, weight
):
    half = depth // 2
    side = where_ref[2]
    weight[pl.ds(pl.multiple_of(side * half, half), half), :] = held_ref[...]
    weight[pl.ds(pl.multiple_of((1 - side) * half, half), half), :] = other_ref[...]
    turn = s0.shape[1] // depth - 1
    rows = s0.shape[0]
    total = total_ref[...] + jnp.dot(
        stacked((s0, s1, s2, s3), turn, depth), weight[...], preferred_element_type=jnp.float32
    )
    keep_ref[0] = total[:rows]
    out_ref[0] = total[rows : 2 * rows]
    keep_ref[1] = total[2 * rows : 3 * rows]
    out_ref[1] = total[3 * rows :]


def far_of(where, shares, total, held, other):
    half, columns = held.shape
    rows = shares[0].shape[0]
    result = jax.ShapeDtypeStruct((2, rows, columns), jnp.float32)
    return pl.pallas_call(
        functools.partial(far_kernel, 2 * half),
        in_specs=[SMEM] + [VMEM] * (SQUARE + 3),
        out_specs=[VMEM] * 2,
        out_shape=[result] * 2,
        scratch_shapes=[pltpu.VMEM((2 * half, columns), held.dtype)],
        compiler_params=params(),
        cost_estimate=cost(2 * SQUARE * rows * 2 * half * columns, 2**22),
    )(where, *shares, total, held, other)


def half_kernel(where_ref, whole_ref, half_ref):
    half = half_ref.shape[0]
    start = pl.multiple_of(where_ref[2] * half, half)
    half_ref[...] = whole_ref[pl.ds(start, half), :]


def half_of(where, whole):
    depth, columns = whole.shape
    return pl.pallas_call(
        half_kernel,
        in_specs=[SMEM, VMEM],
        out_specs=VMEM,
        out_shape=jax.ShapeDtypeStruct((depth // 2, columns), whole.dtype),
        compiler_params=params(),
        cost_estimate=cost(0, 3 * depth * columns),
    )(where, whole)


def per_device(
    tokens,
    value_weight_matrix,
    adapter_down_weight,
    adapter_up_weight,
    adapter_of_block,
    block_live_length,
):
    group_count = lax.axis_size("groups")
    peer_count = lax.axis_size("dp")
    ring = peer_count // SQUARE
    depth, columns = value_weight_matrix.shape
    rank, width = adapter_up_weight.shape[1:]
    group, peer = lax.axis_index("groups"), lax.axis_index("dp")
    where = jnp.stack([peer // SQUARE, lax.rem(peer, SQUARE), lax.rem(group, 2)])

    onward = []
    for g in range(group_count):
        for p in range(peer_count):
            place = (p // SQUARE + (1 if g % 2 == 0 else ring - 1)) % ring
            onward.append((g * peer_count + p, g * peer_count + place * SQUARE + p % SQUARE))

    def along(x):
        return lax.ppermute(x, ("groups", "dp"), onward)

    def across(x):
        return lax.ppermute(x, "groups", [(g, g ^ 1) for g in range(group_count)])

    def within(x, step):
        return lax.ppermute(x, "dp", [(p, p ^ step) for p in range(peer_count)])

    wide = columns // CHUNKS
    held = [value_weight_matrix[:, c * wide : (c + 1) * wide] for c in range(CHUNKS)]
    pieces = [[] for _ in range(CHUNKS)]
    for _ in range(ring // 2 - 1):
        for c in range(CHUNKS):
            held[c] = along(held[c])
            pieces[c] += [held[c], across(held[c])]
    far = []
    for c in range(CHUNKS):
        mine = along(half_of(where, held[c]))
        far.append((mine, across(mine)))

    shares = shares_of(where, tokens, ring, depth)
    shares = [shares[0]] + [within(shares[m], m) for m in range(1, SQUARE)]

    packets = packets_of(adapter_of_block, adapter_down_weight, adapter_up_weight)
    packets = lax.all_to_all(packets, "dp", 0, 0, tiled=True)
    change = change_of(tokens, packets, rank, depth, width)

    base = []
    for c in range(CHUNKS):
        total = near_of(shares, value_weight_matrix, c, pieces[c])
        outgoing, keep = far_of(where, shares, total, *far[c])
        incoming = within(outgoing, 1)
        there = within(keep[1] + incoming[1], 2)
        base.append(keep[0] + incoming[0] + there)
    base = jnp.concatenate(base, axis=1)

    live_rows = jnp.arange(BLOCK, dtype=jnp.int32)[None, :] < block_live_length[:, None]
    return jnp.where(live_rows.reshape(-1, 1), base + change, 0.0).astype(jnp.bfloat16)


def solution(mesh):
    in_specs = (
        P(("groups", "dp"), None),
        P("dp", None),
        P(None, None, "dp"),
        P(None, None, "dp"),
        P("groups"),
        P(("groups", "dp")),
    )
    out_specs = P(("groups", "dp"), None)
    return jax.shard_map(
        per_device, mesh=mesh, in_specs=in_specs, out_specs=out_specs, check_vma=False
    )
```

```python
import functools

import jax
import jax.numpy as jnp
from jax import lax
from jax.experimental import pallas as pl
from jax.experimental.pallas import tpu as pltpu
from jax.sharding import PartitionSpec as P

BLOCK = 128
SQUARE = 4
CHUNKS = 2
LANES = 128
ADAPTER_SCALE = 0.5
VMEM_BYTES = 16 * 2**20
TABLE_VMEM_BYTES = 58 * 2**20

VMEM = pl.BlockSpec(memory_space=pltpu.VMEM)
SMEM = pl.BlockSpec(memory_space=pltpu.SMEM)
HBM = pl.BlockSpec(memory_space=pltpu.HBM)


def params(vmem_bytes=VMEM_BYTES):
    return pltpu.CompilerParams(vmem_limit_bytes=vmem_bytes)


def after(*values):
    return lax.optimization_barrier(values)


def cost(flops, touched):
    return pl.CostEstimate(flops=flops, bytes_accessed=touched, transcendentals=0)


def share_kernel(ring, depth, where_ref, tokens_ref, *share_refs):
    place, member, side = where_ref[0], where_ref[1], where_ref[2]
    step = 2 * side - 1
    order = [0]
    for hop in range(1, ring // 2):
        order += [step * hop, -step * hop]
    order.append(ring // 2)
    for turn, ahead in enumerate(order):
        source = lax.rem(place + ahead + ring, ring)
        for mate, share_ref in enumerate(share_refs):
            start = pl.multiple_of((source * SQUARE + (member ^ mate)) * depth, depth)
            share_ref[:, turn * depth : (turn + 1) * depth] = tokens_ref[:, pl.ds(start, depth)]


def shares_of(where, tokens, ring, depth):
    rows, features = tokens.shape
    share = jax.ShapeDtypeStruct((rows, ring * depth), tokens.dtype)
    return pl.pallas_call(
        functools.partial(share_kernel, ring, depth),
        in_specs=[SMEM, VMEM],
        out_specs=[VMEM] * SQUARE,
        out_shape=[share] * SQUARE,
        compiler_params=params(),
        cost_estimate=cost(0, 4 * rows * features),
    )(where, tokens)


def packet_sizes(depth, rank, width):
    folds = min(LANES // width, rank // 16)
    return depth // LANES, folds, rank // folds


def packet_kernel(
    chosen_ref, down_ref, up_ref, packet_ref, down_held, up_held, packed, sems
):
    blocks, rank, depth = down_held.shape
    width = up_held.shape[2]
    groups, folds, high = packet_sizes(depth, rank, width)

    def copies(k):
        a = chosen_ref[k]
        return (
            pltpu.make_async_copy(down_ref.at[a], down_held.at[k], sems.at[0, k]),
            pltpu.make_async_copy(up_ref.at[a], up_held.at[k], sems.at[1, k]),
        )

    for k in range(blocks):
        for copy in copies(k):
            copy.start()
    def packet(k):
        return pltpu.make_async_copy(packed.at[k], packet_ref.at[k], sems.at[2, k])

    for k in range(blocks):
        for copy in copies(k):
            copy.wait()
        for g in range(groups):
            packed[k, g * rank : (g + 1) * rank, :] = down_held[
                k, :, g * LANES : (g + 1) * LANES
            ]
        parts = [up_held[k, f * high : (f + 1) * high, :] for f in range(folds)]
        if folds * width < LANES:
            parts.append(jnp.zeros((high, LANES - folds * width), packet_ref.dtype))
        packed[k, groups * rank :, :] = jnp.concatenate(parts, axis=1)
        packet(k).start()
    for k in range(blocks):
        packet(k).wait()


def packets_of(adapter_of_block, down, up):
    blocks = adapter_of_block.shape[0]
    rank, depth, width = down.shape[1], down.shape[2], up.shape[2]
    groups, _, high = packet_sizes(depth, rank, width)
    tall = groups * rank + high
    return pl.pallas_call(
        packet_kernel,
        in_specs=[SMEM, HBM, HBM],
        out_specs=HBM,
        out_shape=jax.ShapeDtypeStruct((blocks, tall, LANES), down.dtype),
        scratch_shapes=[
            pltpu.VMEM((blocks, rank, depth), down.dtype),
            pltpu.VMEM((blocks, rank, width), up.dtype),
            pltpu.VMEM((blocks, tall, LANES), down.dtype),
            pltpu.SemaphoreType.DMA((3, blocks)),
        ],
        compiler_params=params(TABLE_VMEM_BYTES),
        cost_estimate=cost(0, 4 * blocks * tall * LANES),
    )(adapter_of_block, down, up)


def change_kernel(rank, depth, width, tokens_ref, packet_ref, change_ref, down_held, up_held):
    peers = packet_ref.shape[0]
    groups, folds, high = packet_sizes(depth, rank, width)
    for p in range(peers):
        for g in range(groups):
            start = p * depth + g * LANES
            down_held[:, start : start + LANES] = packet_ref[p, g * rank : (g + 1) * rank, :]
        for f in range(folds):
            up_held[f * high : (f + 1) * high, p * width : (p + 1) * width] = packet_ref[
                p, groups * rank :, f * width : (f + 1) * width
            ]
    shrunk = lax.dot_general(
        tokens_ref[...],
        down_held[...],
        (((1,), (1,)), ((), ())),
        preferred_element_type=jnp.float32,
    )
    low_rank = (shrunk * ADAPTER_SCALE).astype(jnp.bfloat16)
    change_ref[...] = jnp.dot(low_rank, up_held[...], preferred_element_type=jnp.float32)


def change_of(tokens, packets, rank, depth, width):
    rows, features = tokens.shape
    columns = packets.shape[0] * width
    return pl.pallas_call(
        functools.partial(change_kernel, rank, depth, width),
        in_specs=[VMEM, VMEM],
        out_specs=VMEM,
        out_shape=jax.ShapeDtypeStruct((rows, columns), jnp.float32),
        scratch_shapes=[
            pltpu.VMEM((rank, features), tokens.dtype),
            pltpu.VMEM((rank, columns), tokens.dtype),
        ],
        compiler_params=params(),
        cost_estimate=cost(2 * rows * rank * (features + columns), 2 * rows * features),
    )(tokens, packets)


def half_kernel(turn, where_ref, whole_ref, half_ref):
    half = half_ref.shape[0]
    start = pl.multiple_of((where_ref[2] ^ turn) * half, half)
    half_ref[...] = whole_ref[pl.ds(start, half), :]


def half_of(where, whole, turn):
    depth, columns = whole.shape
    return pl.pallas_call(
        functools.partial(half_kernel, turn),
        in_specs=[SMEM, VMEM],
        out_specs=VMEM,
        out_shape=jax.ShapeDtypeStruct((depth // 2, columns), whole.dtype),
        compiler_params=params(),
        cost_estimate=cost(0, 2 * depth * columns),
    )(where, whole)


def stacked(share_refs, turn, depth):
    return jnp.concatenate(
        [share[:, turn * depth : (turn + 1) * depth] for share in share_refs], axis=0
    )


def place_half(weight, side, half_ref):
    half = half_ref.shape[0]
    weight[pl.ds(pl.multiple_of(side * half, half), half), :] = half_ref[...]


def near_kernel(where_ref, s0, s1, s2, s3, own_ref, *refs):
    pieces, total_ref, weight = refs[:-2], refs[-2], refs[-1]
    depth = own_ref.shape[0]
    shares = (s0, s1, s2, s3)
    side = where_ref[2]
    total_ref[...] = jnp.dot(
        stacked(shares, 0, depth), own_ref[...], preferred_element_type=jnp.float32
    )
    for turn in range(len(pieces) // 2):
        first = lax.rem(side + turn, 2)
        place_half(weight, first, pieces[2 * turn])
        place_half(weight, 1 - first, pieces[2 * turn + 1])
        total_ref[...] += jnp.dot(
            stacked(shares, turn + 1, depth), weight[...], preferred_element_type=jnp.float32
        )


def near_of(where, shares, own, pieces):
    depth, columns = own.shape
    rows = shares[0].shape[0] * SQUARE
    turns = 1 + len(pieces) // 2
    return pl.pallas_call(
        near_kernel,
        in_specs=[SMEM] + [VMEM] * (SQUARE + 1 + len(pieces)),
        out_specs=VMEM,
        out_shape=jax.ShapeDtypeStruct((rows, columns), jnp.float32),
        scratch_shapes=[pltpu.VMEM((depth, columns), own.dtype)],
        compiler_params=params(),
        cost_estimate=cost(2 * rows * depth * columns * turns, 2 * depth * columns * turns),
    )(where, *shares, own, *pieces)


def far_kernel(
    chunk, where_ref, s0, s1, s2, s3, total_ref, mine_ref, other_ref, out_ref, keep_ref, weight
):
    half, wide = mine_ref.shape
    columns = slice(chunk * wide, (chunk + 1) * wide)
    side = where_ref[2]
    place_half(weight, side, mine_ref)
    place_half(weight, 1 - side, other_ref)
    turn = s0.shape[1] // (2 * half) - 1
    rows = s0.shape[0]
    total = total_ref[:, columns] + jnp.dot(
        stacked((s0, s1, s2, s3), turn, 2 * half), weight[...], preferred_element_type=jnp.float32
    )
    keep_ref[0] = total[:rows]
    out_ref[0] = total[rows : 2 * rows]
    keep_ref[1] = total[2 * rows : 3 * rows]
    out_ref[1] = total[3 * rows :]


def far_of(where, shares, total, mine, other, chunk):
    half, wide = mine.shape
    rows = shares[0].shape[0]
    result = jax.ShapeDtypeStruct((2, rows, wide), jnp.float32)
    return pl.pallas_call(
        functools.partial(far_kernel, chunk),
        in_specs=[SMEM] + [VMEM] * (SQUARE + 3),
        out_specs=[VMEM] * 2,
        out_shape=[result] * 2,
        scratch_shapes=[pltpu.VMEM((2 * half, wide), mine.dtype)],
        compiler_params=params(),
        cost_estimate=cost(2 * SQUARE * rows * 2 * half * wide, 2**22),
    )(where, *shares, total, mine, other)


def per_device(
    tokens,
    value_weight_matrix,
    adapter_down_weight,
    adapter_up_weight,
    adapter_of_block,
    block_live_length,
):
    group_count = lax.axis_size("groups")
    peer_count = lax.axis_size("dp")
    ring = peer_count // SQUARE
    depth, columns = value_weight_matrix.shape
    rank, width = adapter_up_weight.shape[1:]
    group, peer = lax.axis_index("groups"), lax.axis_index("dp")
    where = jnp.stack([peer // SQUARE, lax.rem(peer, SQUARE), lax.rem(group, 2)])

    onward = []
    for g in range(group_count):
        for p in range(peer_count):
            place = (p // SQUARE + (1 if g % 2 == 0 else ring - 1)) % ring
            onward.append((g * peer_count + p, g * peer_count + place * SQUARE + p % SQUARE))

    def along(x):
        return lax.ppermute(x, ("groups", "dp"), onward)

    def across(x):
        return lax.ppermute(x, "groups", [(g, g ^ 1) for g in range(group_count)])

    def within(x, step):
        return lax.ppermute(x, "dp", [(p, p ^ step) for p in range(peer_count)])

    held = [half_of(where, value_weight_matrix, turn) for turn in range(2)]
    shares = list(shares_of(where, tokens, ring, depth))
    packets = packets_of(adapter_of_block, adapter_down_weight, adapter_up_weight)
    shares[1], packets = after(shares[1], packets)
    for m in range(1, SQUARE - 1):
        shares[m] = within(shares[m], m)

    pieces = []
    for hop in range(ring // 2 - 1):
        held = [along(piece) for piece in held]
        if hop == 0:
            held[0], shares[1] = after(held[0], shares[1])
            held[1], shares[-1] = after(held[1], shares[-1])
        pieces += held + [across(piece) for piece in held]
    mine = along(held[0])
    shares[-1] = within(shares[-1], SQUARE - 1)

    if pieces:
        packets, pieces[-3] = after(packets, pieces[-3])
    packets = lax.all_to_all(packets, "dp", 0, 0, tiled=True)
    change = change_of(tokens, packets, rank, depth, width)

    total = near_of(where, shares, value_weight_matrix, pieces)
    wide = columns // CHUNKS
    base = []
    for c in range(CHUNKS):
        part = mine[:, c * wide : (c + 1) * wide]
        outgoing, keep = far_of(where, shares, total, part, across(part), c)
        incoming = within(outgoing, 1)
        there = within(keep[1] + incoming[1], 2)
        base.append(keep[0] + incoming[0] + there)
    base = jnp.concatenate(base, axis=1)

    live_rows = jnp.arange(BLOCK, dtype=jnp.int32)[None, :] < block_live_length[:, None]
    return jnp.where(live_rows.reshape(-1, 1), base + change, 0.0).astype(jnp.bfloat16)


def solution(mesh):
    in_specs = (
        P(("groups", "dp"), None),
        P("dp", None),
        P(None, None, "dp"),
        P(None, None, "dp"),
        P("groups"),
        P(("groups", "dp")),
    )
    out_specs = P(("groups", "dp"), None)
    return jax.shard_map(
        per_device, mesh=mesh, in_specs=in_specs, out_specs=out_specs, check_vma=False
    )
```

```python
import functools

import jax
import jax.numpy as jnp
from jax import lax
from jax.experimental import pallas as pl
from jax.experimental.pallas import tpu as pltpu
from jax.sharding import PartitionSpec as P

BLOCK = 128
SQUARE = 4
LANES = 128
ADAPTER_SCALE = 0.5
VMEM_BYTES = 16 * 2**20
TABLE_VMEM_BYTES = 58 * 2**20

VMEM = pl.BlockSpec(memory_space=pltpu.VMEM)
SMEM = pl.BlockSpec(memory_space=pltpu.SMEM)
HBM = pl.BlockSpec(memory_space=pltpu.HBM)


def params(vmem_bytes=VMEM_BYTES):
    return pltpu.CompilerParams(vmem_limit_bytes=vmem_bytes)


def after(*values):
    return lax.optimization_barrier(values)


def cost(flops, touched):
    return pl.CostEstimate(flops=flops, bytes_accessed=touched, transcendentals=0)


def share_kernel(ring, depth, where_ref, tokens_ref, *share_refs):
    place, member, side = where_ref[0], where_ref[1], where_ref[2]
    step = 2 * side - 1
    order = [0]
    for hop in range(1, ring // 2):
        order += [step * hop, -step * hop]
    order.append(ring // 2)
    for turn, ahead in enumerate(order):
        source = lax.rem(place + ahead + ring, ring)
        for mate, share_ref in enumerate(share_refs):
            start = pl.multiple_of((source * SQUARE + (member ^ mate)) * depth, depth)
            share_ref[:, turn * depth : (turn + 1) * depth] = tokens_ref[:, pl.ds(start, depth)]


def shares_of(where, tokens, ring, depth):
    rows, features = tokens.shape
    share = jax.ShapeDtypeStruct((rows, ring * depth), tokens.dtype)
    return pl.pallas_call(
        functools.partial(share_kernel, ring, depth),
        in_specs=[SMEM, VMEM],
        out_specs=[VMEM] * SQUARE,
        out_shape=[share] * SQUARE,
        compiler_params=params(),
        cost_estimate=cost(0, 4 * rows * features),
    )(where, tokens)


def packet_sizes(depth, rank, width):
    folds = min(LANES // width, rank // 16)
    return depth // LANES, folds, rank // folds


def packet_kernel(
    chosen_ref, down_ref, up_ref, packet_ref, down_held, up_held, packed, sems
):
    blocks, rank, depth = down_held.shape
    width = up_held.shape[2]
    groups, folds, high = packet_sizes(depth, rank, width)

    def copies(k):
        a = chosen_ref[k]
        return (
            pltpu.make_async_copy(down_ref.at[a], down_held.at[k], sems.at[0, k]),
            pltpu.make_async_copy(up_ref.at[a], up_held.at[k], sems.at[1, k]),
        )

    for k in range(blocks):
        for copy in copies(k):
            copy.start()
    def packet(k):
        return pltpu.make_async_copy(packed.at[k], packet_ref.at[k], sems.at[2, k])

    for k in range(blocks):
        for copy in copies(k):
            copy.wait()
        for g in range(groups):
            packed[k, g * rank : (g + 1) * rank, :] = down_held[
                k, :, g * LANES : (g + 1) * LANES
            ]
        parts = [up_held[k, f * high : (f + 1) * high, :] for f in range(folds)]
        if folds * width < LANES:
            parts.append(jnp.zeros((high, LANES - folds * width), packet_ref.dtype))
        packed[k, groups * rank :, :] = jnp.concatenate(parts, axis=1)
        packet(k).start()
    for k in range(blocks):
        packet(k).wait()


def packets_of(adapter_of_block, down, up):
    blocks = adapter_of_block.shape[0]
    rank, depth, width = down.shape[1], down.shape[2], up.shape[2]
    groups, _, high = packet_sizes(depth, rank, width)
    tall = groups * rank + high
    return pl.pallas_call(
        packet_kernel,
        in_specs=[SMEM, HBM, HBM],
        out_specs=HBM,
        out_shape=jax.ShapeDtypeStruct((blocks, tall, LANES), down.dtype),
        scratch_shapes=[
            pltpu.VMEM((blocks, rank, depth), down.dtype),
            pltpu.VMEM((blocks, rank, width), up.dtype),
            pltpu.VMEM((blocks, tall, LANES), down.dtype),
            pltpu.SemaphoreType.DMA((3, blocks)),
        ],
        compiler_params=params(TABLE_VMEM_BYTES),
        cost_estimate=cost(0, 4 * blocks * tall * LANES),
    )(adapter_of_block, down, up)


def change_kernel(rank, depth, width, tokens_ref, packet_ref, change_ref, down_held, up_held):
    peers = packet_ref.shape[0]
    groups, folds, high = packet_sizes(depth, rank, width)
    for p in range(peers):
        for g in range(groups):
            start = p * depth + g * LANES
            down_held[:, start : start + LANES] = packet_ref[p, g * rank : (g + 1) * rank, :]
        for f in range(folds):
            up_held[f * high : (f + 1) * high, p * width : (p + 1) * width] = packet_ref[
                p, groups * rank :, f * width : (f + 1) * width
            ]
    shrunk = lax.dot_general(
        tokens_ref[...],
        down_held[...],
        (((1,), (1,)), ((), ())),
        preferred_element_type=jnp.float32,
    )
    low_rank = (shrunk * ADAPTER_SCALE).astype(jnp.bfloat16)
    change_ref[...] = jnp.dot(low_rank, up_held[...], preferred_element_type=jnp.float32)


def change_of(tokens, packets, rank, depth, width):
    rows, features = tokens.shape
    columns = packets.shape[0] * width
    return pl.pallas_call(
        functools.partial(change_kernel, rank, depth, width),
        in_specs=[VMEM, VMEM],
        out_specs=VMEM,
        out_shape=jax.ShapeDtypeStruct((rows, columns), jnp.float32),
        scratch_shapes=[
            pltpu.VMEM((rank, features), tokens.dtype),
            pltpu.VMEM((rank, columns), tokens.dtype),
        ],
        compiler_params=params(),
        cost_estimate=cost(2 * rows * rank * (features + columns), 4 * rows * features),
    )(tokens, packets)


def half_kernel(turn, where_ref, whole_ref, half_ref):
    half = half_ref.shape[0]
    start = pl.multiple_of((where_ref[2] ^ turn) * half, half)
    half_ref[...] = whole_ref[pl.ds(start, half), :]


def half_of(where, whole, turn):
    depth, columns = whole.shape
    return pl.pallas_call(
        functools.partial(half_kernel, turn),
        in_specs=[SMEM, VMEM],
        out_specs=VMEM,
        out_shape=jax.ShapeDtypeStruct((depth // 2, columns), whole.dtype),
        compiler_params=params(),
        cost_estimate=cost(0, 2 * depth * columns),
    )(where, whole)


def stacked(share_refs, turn, depth):
    return jnp.concatenate(
        [share[:, turn * depth : (turn + 1) * depth] for share in share_refs], axis=0
    )


def place_half(weight, side, half_ref):
    half = half_ref.shape[0]
    weight[pl.ds(pl.multiple_of(side * half, half), half), :] = half_ref[...]


def near_kernel(where_ref, s0, s1, s2, s3, own_ref, mine_ref, *refs):
    pieces, (total_ref, left_ref, weight) = refs[:-3], refs[-3:]
    depth = weight.shape[0]
    half = depth // 2
    shares = (s0, s1, s2, s3)
    side = where_ref[2]
    total_ref[...] = jnp.dot(
        stacked(shares, 0, depth), own_ref[...], preferred_element_type=jnp.float32
    )
    turns = len(pieces) // 2
    for turn in range(turns):
        first = lax.rem(side + turn, 2)
        place_half(weight, first, pieces[2 * turn])
        place_half(weight, 1 - first, pieces[2 * turn + 1])
        total_ref[...] += jnp.dot(
            stacked(shares, turn + 1, depth), weight[...], preferred_element_type=jnp.float32
        )
    far = stacked(shares, turns + 1, depth)
    low, high = far[:, :half], far[:, half:]
    total_ref[...] += jnp.dot(
        jnp.where(side == 0, low, high), mine_ref[...], preferred_element_type=jnp.float32
    )
    left_ref[...] = jnp.where(side == 0, high, low)


def near_of(where, shares, own, mine, pieces):
    depth, columns = own.shape
    rows = shares[0].shape[0] * SQUARE
    return pl.pallas_call(
        near_kernel,
        in_specs=[SMEM] + [VMEM] * (SQUARE + 2 + len(pieces)),
        out_specs=[VMEM] * 2,
        out_shape=[
            jax.ShapeDtypeStruct((rows, columns), jnp.float32),
            jax.ShapeDtypeStruct((rows, depth // 2), own.dtype),
        ],
        scratch_shapes=[pltpu.VMEM((depth, columns), own.dtype)],
        compiler_params=params(),
        cost_estimate=cost(2 * rows * depth * columns * (1 + len(pieces) // 2), 8 * rows * columns),
    )(where, *shares, own, mine, *pieces)


def far_kernel(total_ref, left_ref, other_ref, out_ref, keep_ref):
    rows = out_ref.shape[1]
    total = total_ref[...] + jnp.dot(
        left_ref[...], other_ref[...], preferred_element_type=jnp.float32
    )
    keep_ref[0] = total[:rows]
    out_ref[0] = total[rows : 2 * rows]
    keep_ref[1] = total[2 * rows : 3 * rows]
    out_ref[1] = total[3 * rows :]


def far_of(total, left, other):
    rows, columns = total.shape[0] // SQUARE, other.shape[1]
    result = jax.ShapeDtypeStruct((2, rows, columns), jnp.float32)
    return pl.pallas_call(
        far_kernel,
        in_specs=[VMEM] * 3,
        out_specs=[VMEM] * 2,
        out_shape=[result] * 2,
        compiler_params=params(),
        cost_estimate=cost(8 * rows * left.shape[1] * columns, 32 * rows * columns),
    )(total, left, other)


def per_device(
    tokens,
    value_weight_matrix,
    adapter_down_weight,
    adapter_up_weight,
    adapter_of_block,
    block_live_length,
):
    group_count = lax.axis_size("groups")
    peer_count = lax.axis_size("dp")
    ring = peer_count // SQUARE
    depth, columns = value_weight_matrix.shape
    rank, width = adapter_up_weight.shape[1:]
    group, peer = lax.axis_index("groups"), lax.axis_index("dp")
    where = jnp.stack([peer // SQUARE, lax.rem(peer, SQUARE), lax.rem(group, 2)])

    onward = []
    for g in range(group_count):
        for p in range(peer_count):
            place = (p // SQUARE + (1 if g % 2 == 0 else ring - 1)) % ring
            onward.append((g * peer_count + p, g * peer_count + place * SQUARE + p % SQUARE))

    def along(x):
        return lax.ppermute(x, ("groups", "dp"), onward)

    def across(x):
        return lax.ppermute(x, "groups", [(g, g ^ 1) for g in range(group_count)])

    def within(x, step):
        return lax.ppermute(x, "dp", [(p, p ^ step) for p in range(peer_count)])

    held = [half_of(where, value_weight_matrix, turn) for turn in range(2)]
    shares = shares_of(where, tokens, ring, depth)
    packets = packets_of(adapter_of_block, adapter_down_weight, adapter_up_weight)

    swapped, packets = after(shares[1], packets)
    swapped, crossed, slanted = within(swapped, 1), within(shares[2], 2), shares[3]
    pieces = []
    for hop in range(ring // 2 - 1):
        held = [along(piece) for piece in held]
        if hop == 0:
            held[0], swapped = after(held[0], swapped)
            held[1], slanted = after(held[1], slanted)
            held[1], packets = after(held[1], packets)
        pieces += held + [across(piece) for piece in held]
    mine = along(held[0])
    shares = [shares[0], swapped, crossed, within(slanted, 3)]
    packets = lax.all_to_all(packets, "dp", 0, 0, tiled=True)

    total, left = near_of(where, shares, value_weight_matrix, mine, pieces)
    outgoing, keep = far_of(total, left, across(mine))
    incoming = within(outgoing, 1)
    there = (keep[1] + incoming[1]).astype(jnp.bfloat16)
    base = keep[0] + incoming[0] + within(there, 2).astype(jnp.float32)

    change = change_of(tokens, packets, rank, depth, width)
    live_rows = jnp.arange(BLOCK, dtype=jnp.int32)[None, :] < block_live_length[:, None]
    return jnp.where(live_rows.reshape(-1, 1), base + change, 0.0).astype(jnp.bfloat16)


def solution(mesh):
    in_specs = (
        P(("groups", "dp"), None),
        P("dp", None),
        P(None, None, "dp"),
        P(None, None, "dp"),
        P("groups"),
        P(("groups", "dp")),
    )
    out_specs = P(("groups", "dp"), None)
    return jax.shard_map(
        per_device, mesh=mesh, in_specs=in_specs, out_specs=out_specs, check_vma=False
    )
```

```python
import functools

import jax
import jax.numpy as jnp
from jax import lax
from jax.experimental import pallas as pl
from jax.experimental.pallas import tpu as pltpu
from jax.sharding import PartitionSpec as P

BLOCK = 128
SQUARE = 4
WORK = {
    "half": 0.0,
    "share": 4.0,
    "packet": 0.0,
    "near": 16.0,
    "far": 0.1,
    "join": 2.0,
    "change": 2.0,
}
LANES = 128
ADAPTER_SCALE = 0.5
VMEM_BYTES = 16 * 2**20
TABLE_VMEM_BYTES = 58 * 2**20

VMEM = pl.BlockSpec(memory_space=pltpu.VMEM)
SMEM = pl.BlockSpec(memory_space=pltpu.SMEM)
HBM = pl.BlockSpec(memory_space=pltpu.HBM)


def params(vmem_bytes=VMEM_BYTES):
    return pltpu.CompilerParams(vmem_limit_bytes=vmem_bytes)


def after(*values):
    return lax.optimization_barrier(values)


def cost(step, touched):
    flops = int(WORK[step] * 1e9)
    return pl.CostEstimate(flops=flops, bytes_accessed=touched, transcendentals=0)


def share_kernel(ring, depth, where_ref, tokens_ref, *share_refs):
    place, member, side = where_ref[0], where_ref[1], where_ref[2]
    step = 2 * side - 1
    order = [0]
    for hop in range(1, ring // 2):
        order += [step * hop, -step * hop]
    order.append(ring // 2)
    for turn, ahead in enumerate(order):
        source = lax.rem(place + ahead + ring, ring)
        for mate, share_ref in enumerate(share_refs):
            start = pl.multiple_of((source * SQUARE + (member ^ mate)) * depth, depth)
            share_ref[:, turn * depth : (turn + 1) * depth] = tokens_ref[:, pl.ds(start, depth)]


def shares_of(where, tokens, ring, depth):
    rows, features = tokens.shape
    share = jax.ShapeDtypeStruct((rows, ring * depth), tokens.dtype)
    return pl.pallas_call(
        functools.partial(share_kernel, ring, depth),
        in_specs=[SMEM, VMEM],
        out_specs=[VMEM] * SQUARE,
        out_shape=[share] * SQUARE,
        compiler_params=params(),
        cost_estimate=cost("share", 4 * rows * features),
    )(where, tokens)


def packet_sizes(depth, rank, width):
    folds = min(LANES // width, rank // 16)
    return depth // LANES, folds, rank // folds


def packet_kernel(
    chosen_ref, down_ref, up_ref, packet_ref, down_held, up_held, packed, sems
):
    blocks, rank, depth = down_held.shape
    width = up_held.shape[2]
    groups, folds, high = packet_sizes(depth, rank, width)

    def copies(k):
        a = chosen_ref[k]
        return (
            pltpu.make_async_copy(down_ref.at[a], down_held.at[k], sems.at[0, k]),
            pltpu.make_async_copy(up_ref.at[a], up_held.at[k], sems.at[1, k]),
        )

    for k in range(blocks):
        for copy in copies(k):
            copy.start()
    def packet(k):
        return pltpu.make_async_copy(packed.at[k], packet_ref.at[k], sems.at[2, k])

    for k in range(blocks):
        for copy in copies(k):
            copy.wait()
        for g in range(groups):
            packed[k, g * rank : (g + 1) * rank, :] = down_held[
                k, :, g * LANES : (g + 1) * LANES
            ]
        parts = [up_held[k, f * high : (f + 1) * high, :] for f in range(folds)]
        if folds * width < LANES:
            parts.append(jnp.zeros((high, LANES - folds * width), packet_ref.dtype))
        packed[k, groups * rank :, :] = jnp.concatenate(parts, axis=1)
        packet(k).start()
    for k in range(blocks):
        packet(k).wait()


def packets_of(adapter_of_block, down, up):
    blocks = adapter_of_block.shape[0]
    rank, depth, width = down.shape[1], down.shape[2], up.shape[2]
    groups, _, high = packet_sizes(depth, rank, width)
    tall = groups * rank + high
    return pl.pallas_call(
        packet_kernel,
        in_specs=[SMEM, HBM, HBM],
        out_specs=HBM,
        out_shape=jax.ShapeDtypeStruct((blocks, tall, LANES), down.dtype),
        scratch_shapes=[
            pltpu.VMEM((blocks, rank, depth), down.dtype),
            pltpu.VMEM((blocks, rank, width), up.dtype),
            pltpu.VMEM((blocks, tall, LANES), down.dtype),
            pltpu.SemaphoreType.DMA((3, blocks)),
        ],
        compiler_params=params(TABLE_VMEM_BYTES),
        cost_estimate=cost("packet", 4 * blocks * tall * LANES),
    )(adapter_of_block, down, up)


def change_kernel(rank, depth, width, tokens_ref, packet_ref, change_ref, down_held, up_held):
    peers = packet_ref.shape[0]
    groups, folds, high = packet_sizes(depth, rank, width)
    for p in range(peers):
        for g in range(groups):
            start = p * depth + g * LANES
            down_held[:, start : start + LANES] = packet_ref[p, g * rank : (g + 1) * rank, :]
        for f in range(folds):
            up_held[f * high : (f + 1) * high, p * width : (p + 1) * width] = packet_ref[
                p, groups * rank :, f * width : (f + 1) * width
            ]
    shrunk = lax.dot_general(
        tokens_ref[...],
        down_held[...],
        (((1,), (1,)), ((), ())),
        preferred_element_type=jnp.float32,
    )
    low_rank = (shrunk * ADAPTER_SCALE).astype(jnp.bfloat16)
    change_ref[...] = jnp.dot(low_rank, up_held[...], preferred_element_type=jnp.float32)


def change_of(tokens, packets, rank, depth, width):
    rows, features = tokens.shape
    columns = packets.shape[0] * width
    return pl.pallas_call(
        functools.partial(change_kernel, rank, depth, width),
        in_specs=[VMEM, VMEM],
        out_specs=VMEM,
        out_shape=jax.ShapeDtypeStruct((rows, columns), jnp.float32),
        scratch_shapes=[
            pltpu.VMEM((rank, features), tokens.dtype),
            pltpu.VMEM((rank, columns), tokens.dtype),
        ],
        compiler_params=params(),
        cost_estimate=cost("change", 4 * rows * features),
    )(tokens, packets)


def half_kernel(turn, where_ref, whole_ref, half_ref):
    half = half_ref.shape[0]
    start = pl.multiple_of((where_ref[2] ^ turn) * half, half)
    half_ref[...] = whole_ref[pl.ds(start, half), :]


def half_of(where, whole, turn):
    depth, columns = whole.shape
    return pl.pallas_call(
        functools.partial(half_kernel, turn),
        in_specs=[SMEM, VMEM],
        out_specs=VMEM,
        out_shape=jax.ShapeDtypeStruct((depth // 2, columns), whole.dtype),
        compiler_params=params(),
        cost_estimate=cost("half", 2 * depth * columns),
    )(where, whole)


def stacked(share_refs, turn, depth):
    return jnp.concatenate(
        [share[:, turn * depth : (turn + 1) * depth] for share in share_refs], axis=0
    )


def place_half(weight, side, half_ref):
    half = half_ref.shape[0]
    weight[pl.ds(pl.multiple_of(side * half, half), half), :] = half_ref[...]


def near_kernel(where_ref, s0, s1, s2, s3, own_ref, mine_ref, *refs):
    pieces, (total_ref, left_ref, weight) = refs[:-3], refs[-3:]
    depth = weight.shape[0]
    half = depth // 2
    shares = (s0, s1, s2, s3)
    side = where_ref[2]
    total_ref[...] = jnp.dot(
        stacked(shares, 0, depth), own_ref[...], preferred_element_type=jnp.float32
    )
    turns = len(pieces) // 2
    for turn in range(turns):
        first = lax.rem(side + turn, 2)
        place_half(weight, first, pieces[2 * turn])
        place_half(weight, 1 - first, pieces[2 * turn + 1])
        total_ref[...] += jnp.dot(
            stacked(shares, turn + 1, depth), weight[...], preferred_element_type=jnp.float32
        )
    far = stacked(shares, turns + 1, depth)
    low, high = far[:, :half], far[:, half:]
    total_ref[...] += jnp.dot(
        jnp.where(side == 0, low, high), mine_ref[...], preferred_element_type=jnp.float32
    )
    left_ref[...] = jnp.where(side == 0, high, low)


def near_of(where, shares, own, mine, pieces):
    depth, columns = own.shape
    rows = shares[0].shape[0] * SQUARE
    return pl.pallas_call(
        near_kernel,
        in_specs=[SMEM] + [VMEM] * (SQUARE + 2 + len(pieces)),
        out_specs=[VMEM] * 2,
        out_shape=[
            jax.ShapeDtypeStruct((rows, columns), jnp.float32),
            jax.ShapeDtypeStruct((rows, depth // 2), own.dtype),
        ],
        scratch_shapes=[pltpu.VMEM((depth, columns), own.dtype)],
        compiler_params=params(),
        cost_estimate=cost("near", 8 * rows * columns),
    )(where, *shares, own, mine, *pieces)


def far_kernel(total_ref, left_ref, other_ref, out_ref, keep_ref):
    rows = out_ref.shape[1]
    total = total_ref[...] + jnp.dot(
        left_ref[...], other_ref[...], preferred_element_type=jnp.float32
    )
    keep_ref[0] = total[:rows]
    out_ref[0] = total[rows : 2 * rows]
    keep_ref[1] = total[2 * rows : 3 * rows]
    out_ref[1] = total[3 * rows :]


def far_of(total, left, other):
    rows, columns = total.shape[0] // SQUARE, other.shape[1]
    result = jax.ShapeDtypeStruct((2, rows, columns), jnp.float32)
    return pl.pallas_call(
        far_kernel,
        in_specs=[VMEM] * 3,
        out_specs=[VMEM] * 2,
        out_shape=[result] * 2,
        compiler_params=params(),
        cost_estimate=cost("far", 32 * rows * columns),
    )(total, left, other)


def join_kernel(keep_ref, incoming_ref, there_ref, here_ref):
    there_ref[...] = (keep_ref[1] + incoming_ref[1]).astype(there_ref.dtype)
    here_ref[...] = keep_ref[0] + incoming_ref[0]


def join_of(keep, incoming):
    rows, columns = keep.shape[1:]
    return pl.pallas_call(
        join_kernel,
        in_specs=[VMEM] * 2,
        out_specs=[VMEM] * 2,
        out_shape=[
            jax.ShapeDtypeStruct((rows, columns), jnp.bfloat16),
            jax.ShapeDtypeStruct((rows, columns), jnp.float32),
        ],
        compiler_params=params(),
        cost_estimate=cost("join", 22 * rows * columns),
    )(keep, incoming)


def per_device(
    tokens,
    value_weight_matrix,
    adapter_down_weight,
    adapter_up_weight,
    adapter_of_block,
    block_live_length,
):
    group_count = lax.axis_size("groups")
    peer_count = lax.axis_size("dp")
    ring = peer_count // SQUARE
    depth, columns = value_weight_matrix.shape
    rank, width = adapter_up_weight.shape[1:]
    group, peer = lax.axis_index("groups"), lax.axis_index("dp")
    where = jnp.stack([peer // SQUARE, lax.rem(peer, SQUARE), lax.rem(group, 2)])

    onward = []
    for g in range(group_count):
        for p in range(peer_count):
            place = (p // SQUARE + (1 if g % 2 == 0 else ring - 1)) % ring
            onward.append((g * peer_count + p, g * peer_count + place * SQUARE + p % SQUARE))

    def along(x):
        return lax.ppermute(x, ("groups", "dp"), onward)

    def across(x):
        return lax.ppermute(x, "groups", [(g, g ^ 1) for g in range(group_count)])

    def within(x, step):
        return lax.ppermute(x, "dp", [(p, p ^ step) for p in range(peer_count)])

    held = [half_of(where, value_weight_matrix, turn) for turn in range(2)]
    shares = shares_of(where, tokens, ring, depth)
    packets = packets_of(adapter_of_block, adapter_down_weight, adapter_up_weight)

    swapped, crossed, slanted = shares[1:]
    swapped, packets = after(swapped, packets)
    swapped, crossed = within(swapped, 1), within(crossed, 2)
    pieces = []
    for hop in range(ring // 2 - 1):
        held = [along(piece) for piece in held]
        if hop == 0:
            held[0], swapped = after(held[0], swapped)
            held[1], slanted, packets = after(held[1], slanted, packets)
        pieces += held + [across(piece) for piece in held]
    mine, crossed = after(along(held[0]), crossed)
    shares = [shares[0], swapped, crossed, within(slanted, 3)]
    packets = lax.all_to_all(packets, "dp", 0, 0, tiled=True)

    total, left = near_of(where, shares, value_weight_matrix, mine, pieces)
    outgoing, keep = far_of(total, left, across(mine))
    incoming = within(outgoing, 1)
    there, here = join_of(keep, incoming)
    base = here + within(there, 2).astype(jnp.float32)

    change = change_of(tokens, packets, rank, depth, width)
    live_rows = jnp.arange(BLOCK, dtype=jnp.int32)[None, :] < block_live_length[:, None]
    return jnp.where(live_rows.reshape(-1, 1), base + change, 0.0).astype(jnp.bfloat16)


def solution(mesh):
    in_specs = (
        P(("groups", "dp"), None),
        P("dp", None),
        P(None, None, "dp"),
        P(None, None, "dp"),
        P("groups"),
        P(("groups", "dp")),
    )
    out_specs = P(("groups", "dp"), None)
    return jax.shard_map(
        per_device, mesh=mesh, in_specs=in_specs, out_specs=out_specs, check_vma=False
    )
```

```python
import functools

import jax
import jax.numpy as jnp
from jax import lax
from jax.experimental import pallas as pl
from jax.experimental.pallas import tpu as pltpu
from jax.sharding import PartitionSpec as P

BLOCK = 128
SQUARE = 4
WORK = {
    "half": 0.0,
    "share": 4.0,
    "packet": 0.0,
    "near": 16.0,
    "far": 0.1,
    "join": 2.0,
    "change": 2.0,
}
LANES = 128
ADAPTER_SCALE = 0.5
VMEM_BYTES = 16 * 2**20
TABLE_VMEM_BYTES = 58 * 2**20

VMEM = pl.BlockSpec(memory_space=pltpu.VMEM)
SMEM = pl.BlockSpec(memory_space=pltpu.SMEM)
HBM = pl.BlockSpec(memory_space=pltpu.HBM)


def params(vmem_bytes=VMEM_BYTES):
    return pltpu.CompilerParams(vmem_limit_bytes=vmem_bytes)


def after(*values):
    return lax.optimization_barrier(values)


def cost(step, touched):
    flops = int(WORK[step] * 1e9)
    return pl.CostEstimate(flops=flops, bytes_accessed=touched, transcendentals=0)


def share_kernel(ring, depth, where_ref, tokens_ref, *share_refs):
    place, member, side = where_ref[0], where_ref[1], where_ref[2]
    step = 2 * side - 1
    order = [0]
    for hop in range(1, ring // 2):
        order += [step * hop, -step * hop]
    order.append(ring // 2)
    for turn, ahead in enumerate(order):
        source = lax.rem(place + ahead + ring, ring)
        for mate, share_ref in enumerate(share_refs):
            start = pl.multiple_of((source * SQUARE + (member ^ mate)) * depth, depth)
            share_ref[:, turn * depth : (turn + 1) * depth] = tokens_ref[:, pl.ds(start, depth)]


def shares_of(where, tokens, ring, depth):
    rows, features = tokens.shape
    share = jax.ShapeDtypeStruct((rows, ring * depth), tokens.dtype)
    return pl.pallas_call(
        functools.partial(share_kernel, ring, depth),
        in_specs=[SMEM, VMEM],
        out_specs=[VMEM] * SQUARE,
        out_shape=[share] * SQUARE,
        compiler_params=params(),
        cost_estimate=cost("share", 4 * rows * features),
    )(where, tokens)


def packet_sizes(depth, rank, width):
    folds = min(LANES // width, rank // 16)
    return depth // LANES, folds, rank // folds


def packet_kernel(
    chosen_ref, down_ref, up_ref, packet_ref, down_held, up_held, packed, sems
):
    blocks, rank, depth = down_held.shape
    width = up_held.shape[2]
    groups, folds, high = packet_sizes(depth, rank, width)

    def copies(k):
        a = chosen_ref[k]
        return (
            pltpu.make_async_copy(down_ref.at[a], down_held.at[k], sems.at[0, k]),
            pltpu.make_async_copy(up_ref.at[a], up_held.at[k], sems.at[1, k]),
        )

    for k in range(blocks):
        for copy in copies(k):
            copy.start()
    def packet(k):
        return pltpu.make_async_copy(packed.at[k], packet_ref.at[k], sems.at[2, k])

    for k in range(blocks):
        for copy in copies(k):
            copy.wait()
        for g in range(groups):
            packed[k, g * rank : (g + 1) * rank, :] = down_held[
                k, :, g * LANES : (g + 1) * LANES
            ]
        parts = [up_held[k, f * high : (f + 1) * high, :] for f in range(folds)]
        if folds * width < LANES:
            parts.append(jnp.zeros((high, LANES - folds * width), packet_ref.dtype))
        packed[k, groups * rank :, :] = jnp.concatenate(parts, axis=1)
        packet(k).start()
    for k in range(blocks):
        packet(k).wait()


def packets_of(adapter_of_block, down, up):
    blocks = adapter_of_block.shape[0]
    rank, depth, width = down.shape[1], down.shape[2], up.shape[2]
    groups, _, high = packet_sizes(depth, rank, width)
    tall = groups * rank + high
    return pl.pallas_call(
        packet_kernel,
        in_specs=[SMEM, HBM, HBM],
        out_specs=HBM,
        out_shape=jax.ShapeDtypeStruct((blocks, tall, LANES), down.dtype),
        scratch_shapes=[
            pltpu.VMEM((blocks, rank, depth), down.dtype),
            pltpu.VMEM((blocks, rank, width), up.dtype),
            pltpu.VMEM((blocks, tall, LANES), down.dtype),
            pltpu.SemaphoreType.DMA((3, blocks)),
        ],
        compiler_params=params(TABLE_VMEM_BYTES),
        cost_estimate=cost("packet", 4 * blocks * tall * LANES),
    )(adapter_of_block, down, up)


def change_kernel(rank, depth, width, tokens_ref, packet_ref, change_ref, down_held, up_held):
    peers = packet_ref.shape[0]
    groups, folds, high = packet_sizes(depth, rank, width)
    for p in range(peers):
        for g in range(groups):
            start = p * depth + g * LANES
            down_held[:, start : start + LANES] = packet_ref[p, g * rank : (g + 1) * rank, :]
        for f in range(folds):
            up_held[f * high : (f + 1) * high, p * width : (p + 1) * width] = packet_ref[
                p, groups * rank :, f * width : (f + 1) * width
            ]
    shrunk = lax.dot_general(
        tokens_ref[...],
        down_held[...],
        (((1,), (1,)), ((), ())),
        preferred_element_type=jnp.float32,
    )
    low_rank = (shrunk * ADAPTER_SCALE).astype(jnp.bfloat16)
    change_ref[...] = jnp.dot(low_rank, up_held[...], preferred_element_type=jnp.float32)


def change_of(tokens, packets, rank, depth, width):
    rows, features = tokens.shape
    columns = packets.shape[0] * width
    return pl.pallas_call(
        functools.partial(change_kernel, rank, depth, width),
        in_specs=[VMEM, VMEM],
        out_specs=VMEM,
        out_shape=jax.ShapeDtypeStruct((rows, columns), jnp.float32),
        scratch_shapes=[
            pltpu.VMEM((rank, features), tokens.dtype),
            pltpu.VMEM((rank, columns), tokens.dtype),
        ],
        compiler_params=params(),
        cost_estimate=cost("change", 4 * rows * features),
    )(tokens, packets)


def half_kernel(turn, where_ref, whole_ref, half_ref):
    half = half_ref.shape[0]
    start = pl.multiple_of((where_ref[2] ^ turn) * half, half)
    half_ref[...] = whole_ref[pl.ds(start, half), :]


def half_of(where, whole, turn):
    depth, columns = whole.shape
    return pl.pallas_call(
        functools.partial(half_kernel, turn),
        in_specs=[SMEM, VMEM],
        out_specs=VMEM,
        out_shape=jax.ShapeDtypeStruct((depth // 2, columns), whole.dtype),
        compiler_params=params(),
        cost_estimate=cost("half", 2 * depth * columns),
    )(where, whole)


def stacked(share_refs, turn, depth):
    return jnp.concatenate(
        [share[:, turn * depth : (turn + 1) * depth] for share in share_refs], axis=0
    )


def place_half(weight, side, half_ref):
    half = half_ref.shape[0]
    weight[pl.ds(pl.multiple_of(side * half, half), half), :] = half_ref[...]


def near_kernel(where_ref, s0, s1, s2, s3, own_ref, mine_ref, *refs):
    pieces, (total_ref, left_ref, weight) = refs[:-3], refs[-3:]
    depth = weight.shape[0]
    half = depth // 2
    shares = (s0, s1, s2, s3)
    side = where_ref[2]
    total_ref[...] = jnp.dot(
        stacked(shares, 0, depth), own_ref[...], preferred_element_type=jnp.float32
    )
    turns = len(pieces) // 2
    for turn in range(turns):
        first = lax.rem(side + turn, 2)
        place_half(weight, first, pieces[2 * turn])
        place_half(weight, 1 - first, pieces[2 * turn + 1])
        total_ref[...] += jnp.dot(
            stacked(shares, turn + 1, depth), weight[...], preferred_element_type=jnp.float32
        )
    far = stacked(shares, turns + 1, depth)
    low, high = far[:, :half], far[:, half:]
    total_ref[...] += jnp.dot(
        jnp.where(side == 0, low, high), mine_ref[...], preferred_element_type=jnp.float32
    )
    left_ref[...] = jnp.where(side == 0, high, low)


def near_of(where, shares, own, mine, pieces):
    depth, columns = own.shape
    rows = shares[0].shape[0] * SQUARE
    return pl.pallas_call(
        near_kernel,
        in_specs=[SMEM] + [VMEM] * (SQUARE + 2 + len(pieces)),
        out_specs=[VMEM] * 2,
        out_shape=[
            jax.ShapeDtypeStruct((rows, columns), jnp.float32),
            jax.ShapeDtypeStruct((rows, depth // 2), own.dtype),
        ],
        scratch_shapes=[pltpu.VMEM((depth, columns), own.dtype)],
        compiler_params=params(),
        cost_estimate=cost("near", 8 * rows * columns),
    )(where, *shares, own, mine, *pieces)


def far_kernel(total_ref, left_ref, other_ref, here_ref, mate_ref, there_ref, past_ref):
    rows = here_ref.shape[0]
    total = total_ref[...] + jnp.dot(
        left_ref[...], other_ref[...], preferred_element_type=jnp.float32
    )
    here_ref[...] = total[:rows]
    mate_ref[...] = total[rows : 2 * rows]
    there_ref[...] = total[2 * rows : 3 * rows]
    past_ref[...] = total[3 * rows :]


def far_of(total, left, other):
    rows, columns = total.shape[0] // SQUARE, other.shape[1]
    result = jax.ShapeDtypeStruct((rows, columns), jnp.float32)
    return pl.pallas_call(
        far_kernel,
        in_specs=[VMEM] * 3,
        out_specs=[VMEM] * SQUARE,
        out_shape=[result] * SQUARE,
        compiler_params=params(),
        cost_estimate=cost("far", 32 * rows * columns),
    )(total, left, other)


def join_kernel(there_ref, past_ref, joined_ref):
    joined_ref[...] = (there_ref[...] + past_ref[...]).astype(joined_ref.dtype)


def join_of(there, past):
    return pl.pallas_call(
        join_kernel,
        in_specs=[VMEM] * 2,
        out_specs=VMEM,
        out_shape=jax.ShapeDtypeStruct(there.shape, jnp.bfloat16),
        compiler_params=params(),
        cost_estimate=cost("join", 10 * there.size),
    )(there, past)


def per_device(
    tokens,
    value_weight_matrix,
    adapter_down_weight,
    adapter_up_weight,
    adapter_of_block,
    block_live_length,
):
    group_count = lax.axis_size("groups")
    peer_count = lax.axis_size("dp")
    ring = peer_count // SQUARE
    depth, columns = value_weight_matrix.shape
    rank, width = adapter_up_weight.shape[1:]
    group, peer = lax.axis_index("groups"), lax.axis_index("dp")
    where = jnp.stack([peer // SQUARE, lax.rem(peer, SQUARE), lax.rem(group, 2)])

    onward = []
    for g in range(group_count):
        for p in range(peer_count):
            place = (p // SQUARE + (1 if g % 2 == 0 else ring - 1)) % ring
            onward.append((g * peer_count + p, g * peer_count + place * SQUARE + p % SQUARE))

    def along(x):
        return lax.ppermute(x, ("groups", "dp"), onward)

    def across(x):
        return lax.ppermute(x, "groups", [(g, g ^ 1) for g in range(group_count)])

    def within(x, step):
        return lax.ppermute(x, "dp", [(p, p ^ step) for p in range(peer_count)])

    held = [half_of(where, value_weight_matrix, turn) for turn in range(2)]
    shares = shares_of(where, tokens, ring, depth)
    packets = packets_of(adapter_of_block, adapter_down_weight, adapter_up_weight)

    swapped, crossed, slanted = shares[1:]
    swapped, packets = after(swapped, packets)
    swapped, crossed = within(swapped, 1), within(crossed, 2)
    pieces = []
    for hop in range(ring // 2 - 1):
        held = [along(piece) for piece in held]
        if hop == 0:
            held[0], swapped = after(held[0], swapped)
            held[1], slanted, packets = after(held[1], slanted, packets)
        pieces += held + [across(piece) for piece in held]
    mine, crossed = after(along(held[0]), crossed)
    shares = [shares[0], swapped, crossed, within(slanted, 3)]
    packets = lax.all_to_all(packets, "dp", 0, 0, tiled=True)

    total, left = near_of(where, shares, value_weight_matrix, mine, pieces)
    here, mate, there, past = far_of(total, left, across(mine))
    joined = within(join_of(there, within(past, 1)), 2)
    base = here + within(mate, 1) + joined.astype(jnp.float32)

    change = change_of(tokens, packets, rank, depth, width)
    live_rows = jnp.arange(BLOCK, dtype=jnp.int32)[None, :] < block_live_length[:, None]
    return jnp.where(live_rows.reshape(-1, 1), base + change, 0.0).astype(jnp.bfloat16)


def solution(mesh):
    in_specs = (
        P(("groups", "dp"), None),
        P("dp", None),
        P(None, None, "dp"),
        P(None, None, "dp"),
        P("groups"),
        P(("groups", "dp")),
    )
    out_specs = P(("groups", "dp"), None)
    return jax.shard_map(
        per_device, mesh=mesh, in_specs=in_specs, out_specs=out_specs, check_vma=False
    )
```

```python
import functools

import jax
import jax.numpy as jnp
from jax import lax
from jax.experimental import pallas as pl
from jax.experimental.pallas import tpu as pltpu
from jax.sharding import PartitionSpec as P

BLOCK = 128
SQUARE = 4
WORK = {
    "half": 0.0,
    "share": 4.0,
    "packet": 0.0,
    "near": 16.0,
    "far": 2.0,
    "join": 8.0,
    "change": 2.0,
}
LANES = 128
ADAPTER_SCALE = 0.5
VMEM_BYTES = 16 * 2**20
TABLE_VMEM_BYTES = 58 * 2**20

VMEM = pl.BlockSpec(memory_space=pltpu.VMEM)
SMEM = pl.BlockSpec(memory_space=pltpu.SMEM)
HBM = pl.BlockSpec(memory_space=pltpu.HBM)


def params(vmem_bytes=VMEM_BYTES):
    return pltpu.CompilerParams(vmem_limit_bytes=vmem_bytes)


def after(*values):
    return lax.optimization_barrier(values)


def cost(step, touched):
    flops = int(WORK[step] * 1e9)
    return pl.CostEstimate(flops=flops, bytes_accessed=touched, transcendentals=0)


def share_kernel(ring, depth, where_ref, tokens_ref, *share_refs):
    place, member, side = where_ref[0], where_ref[1], where_ref[2]
    step = 2 * side - 1
    order = [0]
    for hop in range(1, ring // 2):
        order += [step * hop, -step * hop]
    order.append(ring // 2)
    for turn, ahead in enumerate(order):
        source = lax.rem(place + ahead + ring, ring)
        for mate, share_ref in enumerate(share_refs):
            start = pl.multiple_of((source * SQUARE + (member ^ mate)) * depth, depth)
            share_ref[:, turn * depth : (turn + 1) * depth] = tokens_ref[:, pl.ds(start, depth)]


def shares_of(where, tokens, ring, depth):
    rows, features = tokens.shape
    share = jax.ShapeDtypeStruct((rows, ring * depth), tokens.dtype)
    return pl.pallas_call(
        functools.partial(share_kernel, ring, depth),
        in_specs=[SMEM, VMEM],
        out_specs=[VMEM] * SQUARE,
        out_shape=[share] * SQUARE,
        compiler_params=params(),
        cost_estimate=cost("share", 4 * rows * features),
    )(where, tokens)


def packet_sizes(depth, rank, width):
    folds = min(LANES // width, rank // 16)
    return depth // LANES, folds, rank // folds


def packet_kernel(
    chosen_ref, down_ref, up_ref, packet_ref, down_held, up_held, packed, sems
):
    blocks, rank, depth = down_held.shape
    width = up_held.shape[2]
    groups, folds, high = packet_sizes(depth, rank, width)

    def copies(k):
        a = chosen_ref[k]
        return (
            pltpu.make_async_copy(down_ref.at[a], down_held.at[k], sems.at[0, k]),
            pltpu.make_async_copy(up_ref.at[a], up_held.at[k], sems.at[1, k]),
        )

    for k in range(blocks):
        for copy in copies(k):
            copy.start()
    def packet(k):
        return pltpu.make_async_copy(packed.at[k], packet_ref.at[k], sems.at[2, k])

    for k in range(blocks):
        for copy in copies(k):
            copy.wait()
        for g in range(groups):
            packed[k, g * rank : (g + 1) * rank, :] = down_held[
                k, :, g * LANES : (g + 1) * LANES
            ]
        parts = [up_held[k, f * high : (f + 1) * high, :] for f in range(folds)]
        if folds * width < LANES:
            parts.append(jnp.zeros((high, LANES - folds * width), packet_ref.dtype))
        packed[k, groups * rank :, :] = jnp.concatenate(parts, axis=1)
        packet(k).start()
    for k in range(blocks):
        packet(k).wait()


def packets_of(adapter_of_block, down, up):
    blocks = adapter_of_block.shape[0]
    rank, depth, width = down.shape[1], down.shape[2], up.shape[2]
    groups, _, high = packet_sizes(depth, rank, width)
    tall = groups * rank + high
    return pl.pallas_call(
        packet_kernel,
        in_specs=[SMEM, HBM, HBM],
        out_specs=HBM,
        out_shape=jax.ShapeDtypeStruct((blocks, tall, LANES), down.dtype),
        scratch_shapes=[
            pltpu.VMEM((blocks, rank, depth), down.dtype),
            pltpu.VMEM((blocks, rank, width), up.dtype),
            pltpu.VMEM((blocks, tall, LANES), down.dtype),
            pltpu.SemaphoreType.DMA((3, blocks)),
        ],
        compiler_params=params(TABLE_VMEM_BYTES),
        cost_estimate=cost("packet", 4 * blocks * tall * LANES),
    )(adapter_of_block, down, up)


def change_kernel(rank, depth, width, tokens_ref, packet_ref, change_ref, down_held, up_held):
    peers = packet_ref.shape[0]
    groups, folds, high = packet_sizes(depth, rank, width)
    for p in range(peers):
        for g in range(groups):
            start = p * depth + g * LANES
            down_held[:, start : start + LANES] = packet_ref[p, g * rank : (g + 1) * rank, :]
        for f in range(folds):
            up_held[f * high : (f + 1) * high, p * width : (p + 1) * width] = packet_ref[
                p, groups * rank :, f * width : (f + 1) * width
            ]
    shrunk = lax.dot_general(
        tokens_ref[...],
        down_held[...],
        (((1,), (1,)), ((), ())),
        preferred_element_type=jnp.float32,
    )
    low_rank = (shrunk * ADAPTER_SCALE).astype(jnp.bfloat16)
    change_ref[...] = jnp.dot(low_rank, up_held[...], preferred_element_type=jnp.float32)


def change_of(tokens, packets, rank, depth, width):
    rows, features = tokens.shape
    columns = packets.shape[0] * width
    return pl.pallas_call(
        functools.partial(change_kernel, rank, depth, width),
        in_specs=[VMEM, VMEM],
        out_specs=VMEM,
        out_shape=jax.ShapeDtypeStruct((rows, columns), jnp.float32),
        scratch_shapes=[
            pltpu.VMEM((rank, features), tokens.dtype),
            pltpu.VMEM((rank, columns), tokens.dtype),
        ],
        compiler_params=params(),
        cost_estimate=cost("change", 4 * rows * features),
    )(tokens, packets)


def half_kernel(turn, where_ref, whole_ref, half_ref):
    half = half_ref.shape[0]
    start = pl.multiple_of((where_ref[2] ^ turn) * half, half)
    half_ref[...] = whole_ref[pl.ds(start, half), :]


def half_of(where, whole, turn):
    depth, columns = whole.shape
    return pl.pallas_call(
        functools.partial(half_kernel, turn),
        in_specs=[SMEM, VMEM],
        out_specs=VMEM,
        out_shape=jax.ShapeDtypeStruct((depth // 2, columns), whole.dtype),
        compiler_params=params(),
        cost_estimate=cost("half", 2 * depth * columns),
    )(where, whole)


def stacked(share_refs, turn, depth):
    return jnp.concatenate(
        [share[:, turn * depth : (turn + 1) * depth] for share in share_refs], axis=0
    )


def place_half(weight, side, half_ref):
    half = half_ref.shape[0]
    weight[pl.ds(pl.multiple_of(side * half, half), half), :] = half_ref[...]


def near_kernel(where_ref, s0, s1, s2, s3, own_ref, mine_ref, *refs):
    pieces, (total_ref, left_ref, weight) = refs[:-3], refs[-3:]
    depth = weight.shape[0]
    half = depth // 2
    shares = (s0, s1, s2, s3)
    side = where_ref[2]
    total_ref[...] = jnp.dot(
        stacked(shares, 0, depth), own_ref[...], preferred_element_type=jnp.float32
    )
    turns = len(pieces) // 2
    for turn in range(turns):
        first = lax.rem(side + turn, 2)
        place_half(weight, first, pieces[2 * turn])
        place_half(weight, 1 - first, pieces[2 * turn + 1])
        total_ref[...] += jnp.dot(
            stacked(shares, turn + 1, depth), weight[...], preferred_element_type=jnp.float32
        )
    far = stacked(shares, turns + 1, depth)
    low, high = far[:, :half], far[:, half:]
    total_ref[...] += jnp.dot(
        jnp.where(side == 0, low, high), mine_ref[...], preferred_element_type=jnp.float32
    )
    left_ref[...] = jnp.where(side == 0, high, low)


def near_of(where, shares, own, mine, pieces):
    depth, columns = own.shape
    rows = shares[0].shape[0] * SQUARE
    return pl.pallas_call(
        near_kernel,
        in_specs=[SMEM] + [VMEM] * (SQUARE + 2 + len(pieces)),
        out_specs=[VMEM] * 2,
        out_shape=[
            jax.ShapeDtypeStruct((rows, columns), jnp.float32),
            jax.ShapeDtypeStruct((rows, depth // 2), own.dtype),
        ],
        scratch_shapes=[pltpu.VMEM((depth, columns), own.dtype)],
        compiler_params=params(),
        cost_estimate=cost("near", 8 * rows * columns),
    )(where, *shares, own, mine, *pieces)


def far_kernel(total_ref, left_ref, other_ref, out_ref, keep_ref):
    rows = out_ref.shape[1]
    total = total_ref[...] + jnp.dot(
        left_ref[...], other_ref[...], preferred_element_type=jnp.float32
    )
    keep_ref[0] = total[:rows]
    out_ref[0] = total[rows : 2 * rows]
    keep_ref[1] = total[2 * rows : 3 * rows]
    out_ref[1] = total[3 * rows :]


def far_of(total, left, other):
    rows, columns = total.shape[0] // SQUARE, other.shape[1]
    result = jax.ShapeDtypeStruct((2, rows, columns), jnp.float32)
    return pl.pallas_call(
        far_kernel,
        in_specs=[VMEM] * 3,
        out_specs=[VMEM] * 2,
        out_shape=[result] * 2,
        compiler_params=params(),
        cost_estimate=cost("far", 32 * rows * columns),
    )(total, left, other)


def join_kernel(keep_ref, incoming_ref, there_ref, here_ref):
    there_ref[...] = (keep_ref[1] + incoming_ref[1]).astype(there_ref.dtype)
    here_ref[...] = keep_ref[0] + incoming_ref[0]


def join_of(keep, incoming):
    rows, columns = keep.shape[1:]
    return pl.pallas_call(
        join_kernel,
        in_specs=[VMEM] * 2,
        out_specs=[VMEM] * 2,
        out_shape=[
            jax.ShapeDtypeStruct((rows, columns), jnp.bfloat16),
            jax.ShapeDtypeStruct((rows, columns), jnp.float32),
        ],
        compiler_params=params(),
        cost_estimate=cost("join", 22 * rows * columns),
    )(keep, incoming)


def per_device(
    tokens,
    value_weight_matrix,
    adapter_down_weight,
    adapter_up_weight,
    adapter_of_block,
    block_live_length,
):
    group_count = lax.axis_size("groups")
    peer_count = lax.axis_size("dp")
    ring = peer_count // SQUARE
    depth, columns = value_weight_matrix.shape
    rank, width = adapter_up_weight.shape[1:]
    group, peer = lax.axis_index("groups"), lax.axis_index("dp")
    where = jnp.stack([peer // SQUARE, lax.rem(peer, SQUARE), lax.rem(group, 2)])

    onward = []
    for g in range(group_count):
        for p in range(peer_count):
            place = (p // SQUARE + (1 if g % 2 == 0 else ring - 1)) % ring
            onward.append((g * peer_count + p, g * peer_count + place * SQUARE + p % SQUARE))

    def along(x):
        return lax.ppermute(x, ("groups", "dp"), onward)

    def across(x):
        return lax.ppermute(x, "groups", [(g, g ^ 1) for g in range(group_count)])

    def within(x, step):
        return lax.ppermute(x, "dp", [(p, p ^ step) for p in range(peer_count)])

    held = [half_of(where, value_weight_matrix, turn) for turn in range(2)]
    shares = shares_of(where, tokens, ring, depth)
    packets = packets_of(adapter_of_block, adapter_down_weight, adapter_up_weight)

    swapped, crossed, slanted = shares[1:]
    crossed, packets = after(crossed, packets)
    swapped, crossed = within(swapped, 1), within(crossed, 2)
    pieces = []
    for hop in range(ring // 2 - 1):
        held = [along(piece) for piece in held]
        if hop == 0:
            held[0], swapped = after(held[0], swapped)
            held[1], slanted, packets = after(held[1], slanted, packets)
        pieces += held + [across(piece) for piece in held]
    mine = along(held[0])
    if pieces:
        mine, pieces[-2] = after(mine, pieces[-2])
    shares = [shares[0], swapped, crossed, within(slanted, 3)]
    packets = lax.all_to_all(packets, "dp", 0, 0, tiled=True)

    total, left = near_of(where, shares, value_weight_matrix, mine, pieces)
    outgoing, keep = far_of(total, left, across(mine))
    incoming = within(outgoing, 1)
    there, here = join_of(keep, incoming)
    base = here + within(there, 2).astype(jnp.float32)

    change = change_of(tokens, packets, rank, depth, width)
    live_rows = jnp.arange(BLOCK, dtype=jnp.int32)[None, :] < block_live_length[:, None]
    return jnp.where(live_rows.reshape(-1, 1), base + change, 0.0).astype(jnp.bfloat16)


def solution(mesh):
    in_specs = (
        P(("groups", "dp"), None),
        P("dp", None),
        P(None, None, "dp"),
        P(None, None, "dp"),
        P("groups"),
        P(("groups", "dp")),
    )
    out_specs = P(("groups", "dp"), None)
    return jax.shard_map(
        per_device, mesh=mesh, in_specs=in_specs, out_specs=out_specs, check_vma=False
    )
```

```python
import functools

import jax
import jax.numpy as jnp
from jax import lax
from jax.experimental import pallas as pl
from jax.experimental.pallas import tpu as pltpu
from jax.sharding import PartitionSpec as P

BLOCK = 128
SQUARE = 4
WORK = {
    "half": 0.0,
    "share": 4.0,
    "packet": 0.0,
    "near": 16.0,
    "far": 2.0,
    "join": 8.0,
    "change": 2.0,
}
LANES = 128
ADAPTER_SCALE = 0.5
VMEM_BYTES = 16 * 2**20
TABLE_VMEM_BYTES = 58 * 2**20

VMEM = pl.BlockSpec(memory_space=pltpu.VMEM)
SMEM = pl.BlockSpec(memory_space=pltpu.SMEM)
HBM = pl.BlockSpec(memory_space=pltpu.HBM)


def params(vmem_bytes=VMEM_BYTES):
    return pltpu.CompilerParams(vmem_limit_bytes=vmem_bytes)


def after(*values):
    return lax.optimization_barrier(values)


def cost(step, touched):
    flops = int(WORK[step] * 1e9)
    return pl.CostEstimate(flops=flops, bytes_accessed=touched, transcendentals=0)


def starts_of(where_ref, ring, depth, mate):
    place, member, side = where_ref[0], where_ref[1], where_ref[2]
    step = 2 * side - 1
    order = [0]
    for hop in range(1, ring // 2):
        order += [step * hop, -step * hop]
    order.append(ring // 2)
    sources = [lax.rem(place + ahead + ring, ring) for ahead in order]
    return [pl.multiple_of((s * SQUARE + (member ^ mate)) * depth, depth) for s in sources]


def share_kernel(ring, depth, where_ref, tokens_ref, *share_refs):
    for mate, share_ref in enumerate(share_refs):
        for turn, start in enumerate(starts_of(where_ref, ring, depth, mate + 1)):
            share_ref[:, turn * depth : (turn + 1) * depth] = tokens_ref[:, pl.ds(start, depth)]


def shares_of(where, tokens, ring, depth):
    rows, features = tokens.shape
    share = jax.ShapeDtypeStruct((rows, ring * depth), tokens.dtype)
    return pl.pallas_call(
        functools.partial(share_kernel, ring, depth),
        in_specs=[SMEM, VMEM],
        out_specs=[VMEM] * (SQUARE - 1),
        out_shape=[share] * (SQUARE - 1),
        compiler_params=params(),
        cost_estimate=cost("share", 4 * rows * features),
    )(where, tokens)


def packet_sizes(depth, rank, width):
    folds = min(LANES // width, rank // 16)
    return depth // LANES, folds, rank // folds


def packet_kernel(
    chosen_ref, down_ref, up_ref, packet_ref, down_held, up_held, packed, sems
):
    blocks, rank, depth = down_held.shape
    width = up_held.shape[2]
    groups, folds, high = packet_sizes(depth, rank, width)

    def copies(k):
        a = chosen_ref[k]
        return (
            pltpu.make_async_copy(down_ref.at[a], down_held.at[k], sems.at[0, k]),
            pltpu.make_async_copy(up_ref.at[a], up_held.at[k], sems.at[1, k]),
        )

    for k in range(blocks):
        for copy in copies(k):
            copy.start()
    def packet(k):
        return pltpu.make_async_copy(packed.at[k], packet_ref.at[k], sems.at[2, k])

    for k in range(blocks):
        for copy in copies(k):
            copy.wait()
        for g in range(groups):
            packed[k, g * rank : (g + 1) * rank, :] = down_held[
                k, :, g * LANES : (g + 1) * LANES
            ]
        parts = [up_held[k, f * high : (f + 1) * high, :] for f in range(folds)]
        if folds * width < LANES:
            parts.append(jnp.zeros((high, LANES - folds * width), packet_ref.dtype))
        packed[k, groups * rank :, :] = jnp.concatenate(parts, axis=1)
        packet(k).start()
    for k in range(blocks):
        packet(k).wait()


def packets_of(adapter_of_block, down, up):
    blocks = adapter_of_block.shape[0]
    rank, depth, width = down.shape[1], down.shape[2], up.shape[2]
    groups, _, high = packet_sizes(depth, rank, width)
    tall = groups * rank + high
    return pl.pallas_call(
        packet_kernel,
        in_specs=[SMEM, HBM, HBM],
        out_specs=HBM,
        out_shape=jax.ShapeDtypeStruct((blocks, tall, LANES), down.dtype),
        scratch_shapes=[
            pltpu.VMEM((blocks, rank, depth), down.dtype),
            pltpu.VMEM((blocks, rank, width), up.dtype),
            pltpu.VMEM((blocks, tall, LANES), down.dtype),
            pltpu.SemaphoreType.DMA((3, blocks)),
        ],
        compiler_params=params(TABLE_VMEM_BYTES),
        cost_estimate=cost("packet", 4 * blocks * tall * LANES),
    )(adapter_of_block, down, up)


def change_kernel(rank, depth, width, tokens_ref, packet_ref, change_ref, down_held, up_held):
    peers = packet_ref.shape[0]
    groups, folds, high = packet_sizes(depth, rank, width)
    for p in range(peers):
        for g in range(groups):
            start = p * depth + g * LANES
            down_held[:, start : start + LANES] = packet_ref[p, g * rank : (g + 1) * rank, :]
        for f in range(folds):
            up_held[f * high : (f + 1) * high, p * width : (p + 1) * width] = packet_ref[
                p, groups * rank :, f * width : (f + 1) * width
            ]
    shrunk = lax.dot_general(
        tokens_ref[...],
        down_held[...],
        (((1,), (1,)), ((), ())),
        preferred_element_type=jnp.float32,
    )
    low_rank = (shrunk * ADAPTER_SCALE).astype(jnp.bfloat16)
    change_ref[...] = jnp.dot(low_rank, up_held[...], preferred_element_type=jnp.float32)


def change_of(tokens, packets, rank, depth, width):
    rows, features = tokens.shape
    columns = packets.shape[0] * width
    return pl.pallas_call(
        functools.partial(change_kernel, rank, depth, width),
        in_specs=[VMEM, VMEM],
        out_specs=VMEM,
        out_shape=jax.ShapeDtypeStruct((rows, columns), jnp.float32),
        scratch_shapes=[
            pltpu.VMEM((rank, features), tokens.dtype),
            pltpu.VMEM((rank, columns), tokens.dtype),
        ],
        compiler_params=params(),
        cost_estimate=cost("change", 4 * rows * features),
    )(tokens, packets)


def half_kernel(turn, where_ref, whole_ref, half_ref):
    half = half_ref.shape[0]
    start = pl.multiple_of((where_ref[2] ^ turn) * half, half)
    half_ref[...] = whole_ref[pl.ds(start, half), :]


def half_of(where, whole, turn):
    depth, columns = whole.shape
    return pl.pallas_call(
        functools.partial(half_kernel, turn),
        in_specs=[SMEM, VMEM],
        out_specs=VMEM,
        out_shape=jax.ShapeDtypeStruct((depth // 2, columns), whole.dtype),
        compiler_params=params(),
        cost_estimate=cost("half", 2 * depth * columns),
    )(where, whole)


def stacked(tokens_ref, start, share_refs, turn, depth):
    own = tokens_ref[:, pl.ds(start, depth)]
    others = [share[:, turn * depth : (turn + 1) * depth] for share in share_refs]
    return jnp.concatenate([own] + others, axis=0)


def place_half(weight, side, half_ref):
    half = half_ref.shape[0]
    weight[pl.ds(pl.multiple_of(side * half, half), half), :] = half_ref[...]


def near_kernel(where_ref, tokens_ref, s1, s2, s3, own_ref, mine_ref, *refs):
    pieces, (total_ref, left_ref, weight) = refs[:-3], refs[-3:]
    depth = weight.shape[0]
    half = depth // 2
    shares = (s1, s2, s3)
    side = where_ref[2]
    starts = starts_of(where_ref, s1.shape[1] // depth, depth, 0)
    total_ref[...] = jnp.dot(
        stacked(tokens_ref, starts[0], shares, 0, depth), own_ref[...], preferred_element_type=jnp.float32
    )
    turns = len(pieces) // 2
    for turn in range(turns):
        first = lax.rem(side + turn, 2)
        place_half(weight, first, pieces[2 * turn])
        place_half(weight, 1 - first, pieces[2 * turn + 1])
        total_ref[...] += jnp.dot(
            stacked(tokens_ref, starts[turn + 1], shares, turn + 1, depth), weight[...], preferred_element_type=jnp.float32
        )
    far = stacked(tokens_ref, starts[-1], shares, turns + 1, depth)
    low, high = far[:, :half], far[:, half:]
    total_ref[...] += jnp.dot(
        jnp.where(side == 0, low, high), mine_ref[...], preferred_element_type=jnp.float32
    )
    left_ref[...] = jnp.where(side == 0, high, low)


def near_of(where, tokens, shares, own, mine, pieces):
    depth, columns = own.shape
    rows = tokens.shape[0] * SQUARE
    return pl.pallas_call(
        near_kernel,
        in_specs=[SMEM] + [VMEM] * (SQUARE + 2 + len(pieces)),
        out_specs=[VMEM] * 2,
        out_shape=[
            jax.ShapeDtypeStruct((rows, columns), jnp.float32),
            jax.ShapeDtypeStruct((rows, depth // 2), own.dtype),
        ],
        scratch_shapes=[pltpu.VMEM((depth, columns), own.dtype)],
        compiler_params=params(),
        cost_estimate=cost("near", 8 * rows * columns),
    )(where, tokens, *shares, own, mine, *pieces)


def far_kernel(total_ref, left_ref, other_ref, out_ref, keep_ref):
    rows = out_ref.shape[1]
    total = total_ref[...] + jnp.dot(
        left_ref[...], other_ref[...], preferred_element_type=jnp.float32
    )
    keep_ref[0] = total[:rows]
    out_ref[0] = total[rows : 2 * rows]
    keep_ref[1] = total[2 * rows : 3 * rows]
    out_ref[1] = total[3 * rows :]


def far_of(total, left, other):
    rows, columns = total.shape[0] // SQUARE, other.shape[1]
    result = jax.ShapeDtypeStruct((2, rows, columns), jnp.float32)
    return pl.pallas_call(
        far_kernel,
        in_specs=[VMEM] * 3,
        out_specs=[VMEM] * 2,
        out_shape=[result] * 2,
        compiler_params=params(),
        cost_estimate=cost("far", 32 * rows * columns),
    )(total, left, other)


def join_kernel(keep_ref, incoming_ref, there_ref, here_ref):
    there_ref[...] = (keep_ref[1] + incoming_ref[1]).astype(there_ref.dtype)
    here_ref[...] = keep_ref[0] + incoming_ref[0]


def join_of(keep, incoming):
    rows, columns = keep.shape[1:]
    return pl.pallas_call(
        join_kernel,
        in_specs=[VMEM] * 2,
        out_specs=[VMEM] * 2,
        out_shape=[
            jax.ShapeDtypeStruct((rows, columns), jnp.bfloat16),
            jax.ShapeDtypeStruct((rows, columns), jnp.float32),
        ],
        compiler_params=params(),
        cost_estimate=cost("join", 22 * rows * columns),
    )(keep, incoming)


def per_device(
    tokens,
    value_weight_matrix,
    adapter_down_weight,
    adapter_up_weight,
    adapter_of_block,
    block_live_length,
):
    group_count = lax.axis_size("groups")
    peer_count = lax.axis_size("dp")
    ring = peer_count // SQUARE
    depth, columns = value_weight_matrix.shape
    rank, width = adapter_up_weight.shape[1:]
    group, peer = lax.axis_index("groups"), lax.axis_index("dp")
    where = jnp.stack([peer // SQUARE, lax.rem(peer, SQUARE), lax.rem(group, 2)])

    onward = []
    for g in range(group_count):
        for p in range(peer_count):
            place = (p // SQUARE + (1 if g % 2 == 0 else ring - 1)) % ring
            onward.append((g * peer_count + p, g * peer_count + place * SQUARE + p % SQUARE))

    def along(x):
        return lax.ppermute(x, ("groups", "dp"), onward)

    def across(x):
        return lax.ppermute(x, "groups", [(g, g ^ 1) for g in range(group_count)])

    def within(x, step):
        return lax.ppermute(x, "dp", [(p, p ^ step) for p in range(peer_count)])

    held = [half_of(where, value_weight_matrix, turn) for turn in range(2)]
    shares = shares_of(where, tokens, ring, depth)
    packets = packets_of(adapter_of_block, adapter_down_weight, adapter_up_weight)

    swapped, crossed, slanted = shares
    crossed, packets = after(crossed, packets)
    swapped, crossed = within(swapped, 1), within(crossed, 2)
    pieces = []
    for hop in range(ring // 2 - 1):
        held = [along(piece) for piece in held]
        if hop == 0:
            held[0], swapped = after(held[0], swapped)
            held[1], slanted, packets = after(held[1], slanted, packets)
        pieces += held + [across(piece) for piece in held]
    mine = along(held[0])
    if pieces:
        mine, pieces[-2] = after(mine, pieces[-2])
    shares = [swapped, crossed, within(slanted, 3)]
    packets = lax.all_to_all(packets, "dp", 0, 0, tiled=True)

    total, left = near_of(where, tokens, shares, value_weight_matrix, mine, pieces)
    outgoing, keep = far_of(total, left, across(mine))
    incoming = within(outgoing, 1)
    there, here = join_of(keep, incoming)
    base = here + within(there, 2).astype(jnp.float32)

    change = change_of(tokens, packets, rank, depth, width)
    live_rows = jnp.arange(BLOCK, dtype=jnp.int32)[None, :] < block_live_length[:, None]
    return jnp.where(live_rows.reshape(-1, 1), base + change, 0.0).astype(jnp.bfloat16)


def solution(mesh):
    in_specs = (
        P(("groups", "dp"), None),
        P("dp", None),
        P(None, None, "dp"),
        P(None, None, "dp"),
        P("groups"),
        P(("groups", "dp")),
    )
    out_specs = P(("groups", "dp"), None)
    return jax.shard_map(
        per_device, mesh=mesh, in_specs=in_specs, out_specs=out_specs, check_vma=False
    )
```

```python
import functools

import jax
import jax.numpy as jnp
from jax import lax
from jax.experimental import pallas as pl
from jax.experimental.pallas import tpu as pltpu
from jax.sharding import PartitionSpec as P

BLOCK = 128
SQUARE = 4
WORK = {
    "half": 0.0,
    "share": 4.0,
    "packet": 0.0,
    "near": 16.0,
    "far": 2.0,
    "join": 8.0,
    "change": 2.0,
}
LANES = 128
ADAPTER_SCALE = 0.5
VMEM_BYTES = 16 * 2**20
TABLE_VMEM_BYTES = 58 * 2**20

VMEM = pl.BlockSpec(memory_space=pltpu.VMEM)
SMEM = pl.BlockSpec(memory_space=pltpu.SMEM)
HBM = pl.BlockSpec(memory_space=pltpu.HBM)


def params(vmem_bytes=VMEM_BYTES):
    return pltpu.CompilerParams(vmem_limit_bytes=vmem_bytes)


def after(*values):
    return lax.optimization_barrier(values)


def cost(step, touched):
    flops = int(WORK[step] * 1e9)
    return pl.CostEstimate(flops=flops, bytes_accessed=touched, transcendentals=0)


def share_kernel(ring, depth, where_ref, tokens_ref, *share_refs):
    place, member, side = where_ref[0], where_ref[1], where_ref[2]
    step = 2 * side - 1
    order = [0]
    for hop in range(1, ring // 2):
        order += [step * hop, -step * hop]
    order.append(ring // 2)
    for turn, ahead in enumerate(order):
        source = lax.rem(place + ahead + ring, ring)
        for mate, share_ref in enumerate(share_refs):
            start = pl.multiple_of((source * SQUARE + (member ^ mate)) * depth, depth)
            share_ref[:, turn * depth : (turn + 1) * depth] = tokens_ref[:, pl.ds(start, depth)]


def shares_of(where, tokens, ring, depth):
    rows, features = tokens.shape
    share = jax.ShapeDtypeStruct((rows, ring * depth), tokens.dtype)
    return pl.pallas_call(
        functools.partial(share_kernel, ring, depth),
        in_specs=[SMEM, VMEM],
        out_specs=[VMEM] * SQUARE,
        out_shape=[share] * SQUARE,
        compiler_params=params(),
        cost_estimate=cost("share", 4 * rows * features),
    )(where, tokens)


def packet_sizes(depth, rank, width):
    folds = min(LANES // width, rank // 16)
    return depth // LANES, folds, rank // folds


def packet_kernel(
    chosen_ref, down_ref, up_ref, packet_ref, down_held, up_held, packed, sems
):
    blocks, rank, depth = down_held.shape
    width = up_held.shape[2]
    groups, folds, high = packet_sizes(depth, rank, width)

    def copies(k):
        a = chosen_ref[k]
        return (
            pltpu.make_async_copy(down_ref.at[a], down_held.at[k], sems.at[0, k]),
            pltpu.make_async_copy(up_ref.at[a], up_held.at[k], sems.at[1, k]),
        )

    for k in range(blocks):
        for copy in copies(k):
            copy.start()
    def packet(k):
        return pltpu.make_async_copy(packed.at[k], packet_ref.at[k], sems.at[2, k])

    for k in range(blocks):
        for copy in copies(k):
            copy.wait()
        for g in range(groups):
            packed[k, g * rank : (g + 1) * rank, :] = down_held[
                k, :, g * LANES : (g + 1) * LANES
            ]
        parts = [up_held[k, f * high : (f + 1) * high, :] for f in range(folds)]
        if folds * width < LANES:
            parts.append(jnp.zeros((high, LANES - folds * width), packet_ref.dtype))
        packed[k, groups * rank :, :] = jnp.concatenate(parts, axis=1)
        packet(k).start()
    for k in range(blocks):
        packet(k).wait()


def packets_of(adapter_of_block, down, up):
    blocks = adapter_of_block.shape[0]
    rank, depth, width = down.shape[1], down.shape[2], up.shape[2]
    groups, _, high = packet_sizes(depth, rank, width)
    tall = groups * rank + high
    return pl.pallas_call(
        packet_kernel,
        in_specs=[SMEM, HBM, HBM],
        out_specs=HBM,
        out_shape=jax.ShapeDtypeStruct((blocks, tall, LANES), down.dtype),
        scratch_shapes=[
            pltpu.VMEM((blocks, rank, depth), down.dtype),
            pltpu.VMEM((blocks, rank, width), up.dtype),
            pltpu.VMEM((blocks, tall, LANES), down.dtype),
            pltpu.SemaphoreType.DMA((3, blocks)),
        ],
        compiler_params=params(TABLE_VMEM_BYTES),
        cost_estimate=cost("packet", 4 * blocks * tall * LANES),
    )(adapter_of_block, down, up)


def change_kernel(rank, depth, width, tokens_ref, packet_ref, change_ref, down_held, up_held):
    peers = packet_ref.shape[0]
    groups, folds, high = packet_sizes(depth, rank, width)
    for p in range(peers):
        for g in range(groups):
            start = p * depth + g * LANES
            down_held[:, start : start + LANES] = packet_ref[p, g * rank : (g + 1) * rank, :]
        for f in range(folds):
            up_held[f * high : (f + 1) * high, p * width : (p + 1) * width] = packet_ref[
                p, groups * rank :, f * width : (f + 1) * width
            ]
    shrunk = lax.dot_general(
        tokens_ref[...],
        down_held[...],
        (((1,), (1,)), ((), ())),
        preferred_element_type=jnp.float32,
    )
    low_rank = (shrunk * ADAPTER_SCALE).astype(jnp.bfloat16)
    change_ref[...] = jnp.dot(low_rank, up_held[...], preferred_element_type=jnp.float32)


def change_of(tokens, packets, rank, depth, width):
    rows, features = tokens.shape
    columns = packets.shape[0] * width
    return pl.pallas_call(
        functools.partial(change_kernel, rank, depth, width),
        in_specs=[VMEM, VMEM],
        out_specs=VMEM,
        out_shape=jax.ShapeDtypeStruct((rows, columns), jnp.float32),
        scratch_shapes=[
            pltpu.VMEM((rank, features), tokens.dtype),
            pltpu.VMEM((rank, columns), tokens.dtype),
        ],
        compiler_params=params(),
        cost_estimate=cost("change", 4 * rows * features),
    )(tokens, packets)


def half_kernel(turn, where_ref, whole_ref, half_ref):
    half = half_ref.shape[0]
    start = pl.multiple_of((where_ref[2] ^ turn) * half, half)
    half_ref[...] = whole_ref[pl.ds(start, half), :]


def half_of(where, whole, turn):
    depth, columns = whole.shape
    return pl.pallas_call(
        functools.partial(half_kernel, turn),
        in_specs=[SMEM, VMEM],
        out_specs=VMEM,
        out_shape=jax.ShapeDtypeStruct((depth // 2, columns), whole.dtype),
        compiler_params=params(),
        cost_estimate=cost("half", 2 * depth * columns),
    )(where, whole)


def stacked(share_refs, turn, depth):
    return jnp.concatenate(
        [share[:, turn * depth : (turn + 1) * depth] for share in share_refs], axis=0
    )


def place_half(weight, side, half_ref):
    half = half_ref.shape[0]
    weight[pl.ds(pl.multiple_of(side * half, half), half), :] = half_ref[...]


def near_kernel(where_ref, s0, s1, s2, s3, own_ref, mine_ref, *refs):
    pieces, (total_ref, left_ref, weight) = refs[:-3], refs[-3:]
    depth = weight.shape[0]
    half = depth // 2
    shares = (s0, s1, s2, s3)
    side = where_ref[2]
    total_ref[...] = jnp.dot(
        stacked(shares, 0, depth), own_ref[...], preferred_element_type=jnp.float32
    )
    turns = len(pieces) // 2
    for turn in range(turns):
        first = lax.rem(side + turn, 2)
        place_half(weight, first, pieces[2 * turn])
        place_half(weight, 1 - first, pieces[2 * turn + 1])
        total_ref[...] += jnp.dot(
            stacked(shares, turn + 1, depth), weight[...], preferred_element_type=jnp.float32
        )
    far = stacked(shares, turns + 1, depth)
    low, high = far[:, :half], far[:, half:]
    total_ref[...] += jnp.dot(
        jnp.where(side == 0, low, high), mine_ref[...], preferred_element_type=jnp.float32
    )
    left_ref[...] = jnp.where(side == 0, high, low)


def near_of(where, shares, own, mine, pieces):
    depth, columns = own.shape
    rows = shares[0].shape[0] * SQUARE
    return pl.pallas_call(
        near_kernel,
        in_specs=[SMEM] + [VMEM] * (SQUARE + 2 + len(pieces)),
        out_specs=[VMEM] * 2,
        out_shape=[
            jax.ShapeDtypeStruct((rows, columns), jnp.float32),
            jax.ShapeDtypeStruct((rows, depth // 2), own.dtype),
        ],
        scratch_shapes=[pltpu.VMEM((depth, columns), own.dtype)],
        compiler_params=params(),
        cost_estimate=cost("near", 8 * rows * columns),
    )(where, *shares, own, mine, *pieces)


def far_kernel(total_ref, left_ref, other_ref, out_ref, keep_ref):
    rows = out_ref.shape[1]
    total = total_ref[...] + jnp.dot(
        left_ref[...], other_ref[...], preferred_element_type=jnp.float32
    )
    keep_ref[0] = total[:rows]
    out_ref[0] = total[rows : 2 * rows]
    keep_ref[1] = total[2 * rows : 3 * rows]
    out_ref[1] = total[3 * rows :]


def far_of(total, left, other):
    rows, columns = total.shape[0] // SQUARE, other.shape[1]
    result = jax.ShapeDtypeStruct((2, rows, columns), jnp.float32)
    return pl.pallas_call(
        far_kernel,
        in_specs=[VMEM] * 3,
        out_specs=[VMEM] * 2,
        out_shape=[result] * 2,
        compiler_params=params(),
        cost_estimate=cost("far", 32 * rows * columns),
    )(total, left, other)


def join_kernel(keep_ref, incoming_ref, there_ref, here_ref):
    there_ref[...] = (keep_ref[1] + incoming_ref[1]).astype(there_ref.dtype)
    here_ref[...] = keep_ref[0] + incoming_ref[0]


def join_of(keep, incoming):
    rows, columns = keep.shape[1:]
    return pl.pallas_call(
        join_kernel,
        in_specs=[VMEM] * 2,
        out_specs=[VMEM] * 2,
        out_shape=[
            jax.ShapeDtypeStruct((rows, columns), jnp.bfloat16),
            jax.ShapeDtypeStruct((rows, columns), jnp.float32),
        ],
        compiler_params=params(),
        cost_estimate=cost("join", 22 * rows * columns),
    )(keep, incoming)


def per_device(
    tokens,
    value_weight_matrix,
    adapter_down_weight,
    adapter_up_weight,
    adapter_of_block,
    block_live_length,
):
    group_count = lax.axis_size("groups")
    peer_count = lax.axis_size("dp")
    ring = peer_count // SQUARE
    depth, columns = value_weight_matrix.shape
    rank, width = adapter_up_weight.shape[1:]
    group, peer = lax.axis_index("groups"), lax.axis_index("dp")
    where = jnp.stack([peer // SQUARE, lax.rem(peer, SQUARE), lax.rem(group, 2)])

    onward = []
    for g in range(group_count):
        for p in range(peer_count):
            place = (p // SQUARE + (1 if g % 2 == 0 else ring - 1)) % ring
            onward.append((g * peer_count + p, g * peer_count + place * SQUARE + p % SQUARE))

    def along(x):
        return lax.ppermute(x, ("groups", "dp"), onward)

    def across(x):
        return lax.ppermute(x, "groups", [(g, g ^ 1) for g in range(group_count)])

    def within(x, step):
        return lax.ppermute(x, "dp", [(p, p ^ step) for p in range(peer_count)])

    held = [half_of(where, value_weight_matrix, turn) for turn in range(2)]
    shares = shares_of(where, tokens, ring, depth)
    packets = packets_of(adapter_of_block, adapter_down_weight, adapter_up_weight)

    swapped, crossed, slanted = shares[1:]
    crossed, packets = after(crossed, packets)
    swapped, crossed = within(swapped, 1), within(crossed, 2)
    pieces = []
    for hop in range(ring // 2 - 1):
        held = [along(piece) for piece in held]
        if hop == 0:
            held[0], swapped = after(held[0], swapped)
            held[0], slanted = after(held[0], slanted)
            held[1], packets = after(held[1], packets)
        pieces += held + [across(piece) for piece in held]
    mine = along(held[0])
    if pieces:
        mine, pieces[-2] = after(mine, pieces[-2])
    shares = [shares[0], swapped, crossed, within(slanted, 3)]
    packets = lax.all_to_all(packets, "dp", 0, 0, tiled=True)

    total, left = near_of(where, shares, value_weight_matrix, mine, pieces)
    outgoing, keep = far_of(total, left, across(mine))
    incoming = within(outgoing, 1)
    there, here = join_of(keep, incoming)
    base = here + within(there, 2).astype(jnp.float32)

    change = change_of(tokens, packets, rank, depth, width)
    live_rows = jnp.arange(BLOCK, dtype=jnp.int32)[None, :] < block_live_length[:, None]
    return jnp.where(live_rows.reshape(-1, 1), base + change, 0.0).astype(jnp.bfloat16)


def solution(mesh):
    in_specs = (
        P(("groups", "dp"), None),
        P("dp", None),
        P(None, None, "dp"),
        P(None, None, "dp"),
        P("groups"),
        P(("groups", "dp")),
    )
    out_specs = P(("groups", "dp"), None)
    return jax.shard_map(
        per_device, mesh=mesh, in_specs=in_specs, out_specs=out_specs, check_vma=False
    )
```
